256 devices in a mesh: vis: 32 (over x_hi, z, core), facet: 8 (over y, x_lo).
Axes of the slice: x: 4 (x_hi: 2, x_lo: 2; x = x_hi * 2 + x_lo), y: 4, z: 8, core: 2. Of those that a mesh axis runs over, the one named last changes fastest.
Arguments:
- visibilities: float32 [8, 16384], P(None, 'vis'), may hold values from -6 to 6
- weights: float32 [16384], P('vis'), may hold values from 0.5 to 2
- live_slots: int32 [16384], P('vis'), may hold values from 0 to 1, as said below
- station_p: int32 [16384], P('vis'), may hold values from 0 to 61
- station_q: int32 [16384], P('vis'), may hold values from 0 to 61
- interval: int32 [16384], P('vis'), may hold values from 0 to 127
- cell_row: int32 [16384], replicated, may hold values from 0 to 63
- cell_col: int32 [16384], replicated, may hold values from 0 to 2047
- jones_gains: float32 [8, 8, 128, 62], P('facet', None, 'vis'), may hold values from -1.5 to 1.5
- model_image: float32 [8, 2048, 2048], P('facet', 'vis'), may hold values from -6 to 6
Outputs:
- residual_vis: float32 [8, 16384], P(None, 'vis')
- dirty_image: float32 [8, 2048, 2048], P('facet', 'vis')
The draws below stay inside these ranges and needn't reach their ends.
Inputs may be any that keep to these rules, and one draw needn't show every extreme that they name: `live_slots`: each device's slots are ordered by tile owner, 16 slots an owner, live ones first; in every draw one tile owner receives 16 live slots from every device.
All inputs are finite; a program needn't handle non-finite values.
Results may differ from the reference program's by a relative error of at most 0.00011.
Values sent between devices are 32-bit elements; how exact they have to be, the bound alone decides.
A program may use at most 192 MiB of HBM per device.

```python
import math
import jax
import jax.numpy as jnp
from jax import lax

STATIONS = 62
GRID_SIDE = 2048
SLOT_CAP = 16
FACETS = 8
INTERVALS = 128
TILE_ROWS = 64
SLOTS_DEV = 512
SLOTS = 16384
N_VIS = 32


def draw_live_slots(key, part):
    key = jax.random.fold_in(key, 11)
    first_key, second_key = jax.random.split(key)
    central = jax.random.randint(first_key, (), 0, N_VIS)
    counts = jax.random.randint(second_key, (N_VIS, N_VIS), SLOT_CAP // 4, SLOT_CAP + 1)
    counts = jnp.where(jnp.arange(N_VIS)[None, :] == central, SLOT_CAP, counts)
    places = jnp.arange(SLOT_CAP)
    filled = (places[None, None, :] < counts[:, :, None]).astype(jnp.int32)
    return filled.reshape(SLOTS)


def with_ends(drawn, key, low, high):
    spot = [jax.random.randint(jax.random.fold_in(key, axis), (), 0, length) for axis, length in enumerate(drawn.shape)]
    longest = drawn.shape.index(max(drawn.shape))
    next_to = spot[:longest] + [(spot[longest] + 1) % drawn.shape[longest]] + spot[longest + 1:]
    return drawn.at[tuple(spot)].set(low).at[tuple(next_to)].set(high)


def block_scale(own_key, extent, shards, low, high):
    def one(dim, blocks):
        draws = jax.random.uniform(jax.random.fold_in(jax.random.fold_in(own_key, 6), dim), (blocks,), jnp.float32, low / len(shards), high / len(shards))
        return jnp.repeat(jnp.exp(draws), extent[dim] // blocks).reshape((-1,) + (1,) * (len(extent) - dim - 1))

    loudness = one(*shards[0])
    for cut in shards[1:]:
        loudness = loudness * one(*cut)
    return loudness


def bell_draw(rng, shape, deviation, reach, cuts=(), kind=jnp.bfloat16):
    loudness = block_scale(rng, shape, cuts, -0.22, 0.18) if cuts else 1.0
    drawn = jax.random.normal(rng, shape, jnp.float32) * deviation * loudness
    return jnp.minimum(jnp.maximum(drawn, -reach), reach).astype(kind)


def setup_inputs(seed: int = 0) -> dict:
    seeds = jax.random.split(jax.random.key(seed), 11)
    visibilities = bell_draw(seeds[0], (8, SLOTS), 1.0, 6.0, ((1, 32),), jnp.float32)
    weights = jnp.clip(jnp.exp(math.log(2.0) - 1.3862944 * jax.random.uniform(seeds[1], (SLOTS,), jnp.float32) ** block_scale(seeds[1], (SLOTS,), ((0, 32),), -0.2, 0.2)), 0.5, 2.0)
    live_slots = draw_live_slots(jax.random.fold_in(seeds[10], 71), 0)
    station_p = with_ends(jax.random.randint(seeds[3], (SLOTS,), 0, STATIONS), jax.random.fold_in(seeds[3], 1), 0, STATIONS - 1).astype(jnp.int32)
    station_q = with_ends(jax.random.randint(seeds[4], (SLOTS,), 0, STATIONS), jax.random.fold_in(seeds[4], 1), 0, STATIONS - 1).astype(jnp.int32)
    interval = with_ends(jax.random.randint(seeds[5], (SLOTS,), 0, INTERVALS), jax.random.fold_in(seeds[5], 1), 0, INTERVALS - 1).astype(jnp.int32)
    cell_row = with_ends(jax.random.randint(seeds[6], (SLOTS,), 0, TILE_ROWS), jax.random.fold_in(seeds[6], 1), 0, TILE_ROWS - 1).astype(jnp.int32)
    cell_col = with_ends(jax.random.randint(seeds[7], (SLOTS,), 0, GRID_SIDE), jax.random.fold_in(seeds[7], 1), 0, GRID_SIDE - 1).astype(jnp.int32)
    jones_gains = bell_draw(seeds[8], (FACETS, 8, INTERVALS, STATIONS), 0.25, 1.5, ((0, 8), (2, 32)), jnp.float32)
    model_image = bell_draw(seeds[9], (FACETS, GRID_SIDE, GRID_SIDE), 1.0, 6.0, ((0, 8), (1, 32)), jnp.float32)
    return {"visibilities": visibilities, "weights": weights, "live_slots": live_slots, "station_p": station_p, "station_q": station_q, "interval": interval, "cell_row": cell_row, "cell_col": cell_col, "jones_gains": jones_gains, "model_image": model_image}


def jones_outer(left_jones, right_jones):
    real_rows = []
    imag_rows = []
    for row_a in range(2):
        for row_b in range(2):
            real_sum = 0.0
            imag_sum = 0.0
            for inner in range(2):
                left_re = left_jones[:, row_a * 2 + inner]
                left_im = left_jones[:, 4 + row_a * 2 + inner]
                right_re = right_jones[:, row_b * 2 + inner]
                right_im = right_jones[:, 4 + row_b * 2 + inner]
                real_sum = real_sum + left_re * right_re + left_im * right_im
                imag_sum = imag_sum + left_im * right_re - left_re * right_im
            real_rows.append(real_sum)
            imag_rows.append(imag_sum)
    return jnp.stack(real_rows + imag_rows, axis=1)

def jones_stokes(left_jones, right_jones, resid):
    total_re = 0.0
    total_im = 0.0
    for inner in range(2):
        for row_a in range(2):
            for row_b in range(2):
                left_re = left_jones[:, row_a * 2 + inner]
                left_im = left_jones[:, 4 + row_a * 2 + inner]
                res_re = resid[row_a * 2 + row_b]
                res_im = resid[4 + row_a * 2 + row_b]
                right_re = right_jones[:, row_b * 2 + inner]
                right_im = right_jones[:, 4 + row_b * 2 + inner]
                mid_re = left_re * res_re + left_im * res_im
                mid_im = left_re * res_im - left_im * res_re
                total_re = total_re + mid_re * right_re - mid_im * right_im
                total_im = total_im + mid_re * right_im + mid_im * right_re
    return (0.5 * total_re, 0.5 * total_im)

def predicted_sum(model_vals, outer):
    value_re = model_vals[:, 0][:, None]
    value_im = model_vals[:, 1][:, None]
    outer_re = outer[:, 0:4]
    outer_im = outer[:, 4:8]
    pred_re = lax.optimization_barrier(jnp.sum(value_re * outer_re - value_im * outer_im, axis=0))
    pred_im = lax.optimization_barrier(jnp.sum(value_re * outer_im + value_im * outer_re, axis=0))
    return jnp.concatenate([pred_re, pred_im], axis=0)

def reference(visibilities, weights, live_slots, station_p, station_q, interval, cell_row, cell_col, jones_gains, model_image):
    flat_gains = jones_gains.reshape(FACETS, 8, INTERVALS * STATIONS)
    index_p = (interval * STATIONS + station_p).astype(jnp.int32)
    index_q = (interval * STATIONS + station_q).astype(jnp.int32)
    jones_p = jnp.take(flat_gains, index_p, axis=2)
    jones_q = jnp.take(flat_gains, index_q, axis=2)
    slot_ids = jnp.arange(SLOTS, dtype=jnp.int32)
    owner = slot_ids % SLOTS_DEV // SLOT_CAP
    v_index = owner * TILE_ROWS + cell_row
    flat_index = (cell_col * GRID_SIDE + v_index).astype(jnp.int32)

    def model_values(image):
        spectrum = jnp.fft.fft2(image).reshape(-1)[flat_index] / GRID_SIDE
        return jnp.stack([jnp.real(spectrum), jnp.imag(spectrum)])
    model_vals = lax.map(model_values, model_image)
    outer = jones_outer(jones_p, jones_q)
    predicted = predicted_sum(model_vals, outer)
    live_float = live_slots.astype(jnp.float32)
    residual_vis = (visibilities - predicted) * live_float
    stokes_re, stokes_im = jones_stokes(jones_p, jones_q, residual_vis)
    scale_w = weights * live_float
    stokes = jnp.stack([stokes_re * scale_w, stokes_im * scale_w], axis=1)
    factor = 4.0 / math.sqrt(SLOTS)

    def dirty_one(pair):
        grid_re = jnp.zeros((GRID_SIDE * GRID_SIDE,), jnp.float32).at[flat_index].add(pair[0])
        grid_im = jnp.zeros((GRID_SIDE * GRID_SIDE,), jnp.float32).at[flat_index].add(pair[1])
        field = (grid_re + 1j * grid_im).reshape(GRID_SIDE, GRID_SIDE)
        return jnp.real(jnp.fft.ifft2(field)) * (GRID_SIDE * GRID_SIDE * factor)
    dirty_image = lax.map(dirty_one, stokes)
    return (residual_vis, dirty_image)
```

```python
import functools
import math

import jax
import jax.numpy as jnp
import numpy as np
from jax import lax
from jax.experimental import pallas as pl
from jax.experimental.pallas import tpu as pltpu
from jax.sharding import PartitionSpec as P

TWO_PI = 2.0 * math.pi
MESH = pl.DeviceIdType.MESH
F32 = jnp.float32
BF16 = jnp.bfloat16

RADIX = 16
INNER = 128
SIDE = RADIX * INNER


def split_table(table):
    high = table.astype(BF16)
    low = (table - high.astype(np.float64)).astype(BF16)
    return high, low


def make_tables():
    inner = np.arange(INNER)
    angle = TWO_PI * (np.outer(inner, inner) % INNER) / INNER
    first = np.concatenate([np.cos(angle), -np.sin(angle)], axis=1)
    last = np.concatenate([np.cos(angle), -np.sin(angle)], axis=0)
    twist = TWO_PI * np.outer(np.arange(RADIX), inner) / SIDE
    twist = np.stack([np.cos(twist), np.sin(twist)]).astype(np.float32)
    return split_table(first) + split_table(last) + (twist,)


def split_pair(value):
    high = value.astype(BF16)
    low = (value - high.astype(F32)).astype(BF16)
    return high, low


def matmul(left, right):
    return jnp.dot(left, right, preferred_element_type=F32)


def cmul_const(pair, real, imag):
    re, im = pair
    return re * real - im * imag, re * imag + im * real


def radix4(vals, sign):
    (ar, ai), (br, bi), (cr, ci), (dr, di) = vals
    sr, si = ar + cr, ai + ci
    tr, ti = ar - cr, ai - ci
    ur, ui = br + dr, bi + di
    wr, wi = br - dr, bi - di
    if sign < 0:
        xr, xi = wi, -wr
    else:
        xr, xi = -wi, wr
    return [(sr + ur, si + ui), (tr + xr, ti + xi), (sr - ur, si - ui), (tr - xr, ti - xi)]


def radix16(vals, sign):
    inner = [radix4([vals[4 * n1 + n2] for n1 in range(4)], sign) for n2 in range(4)]
    out = [None] * 16
    for k1 in range(4):
        column = []
        for n2 in range(4):
            turn = n2 * k1
            value = inner[n2][k1]
            if turn == 4:
                re, im = value
                value = (im, -re) if sign < 0 else (-im, re)
            elif turn == 2 or turn == 6:
                half = math.sqrt(0.5)
                re, im = value
                if sign < 0:
                    value = ((re + im) * half, (im - re) * half)
                else:
                    value = ((re - im) * half, (re + im) * half)
                if turn == 6:
                    re, im = value
                    value = (im, -re) if sign < 0 else (-im, re)
            elif turn:
                angle = sign * TWO_PI * turn / 16
                value = cmul_const(value, math.cos(angle), math.sin(angle))
            column.append(value)
        for k2, value in enumerate(radix4(column, sign)):
            out[k1 + 4 * k2] = value
    return out


def unit_phase(step):
    quarter = (step + 256) >> 9
    angle = (step - (quarter << 9)).astype(F32) * (TWO_PI / SIDE)
    square = angle * angle
    sine = angle * (
        1.0
        + square
        * (-1.0 / 6 + square * (1.0 / 120 + square * (-1.0 / 5040 + square * (1.0 / 362880))))
    )
    cosine = 1.0 + square * (
        -0.5 + square * (1.0 / 24 + square * (-1.0 / 720 + square * (1.0 / 40320)))
    )
    odd = (quarter & 1) == 1
    cos_mag = jnp.where(odd, sine, cosine)
    sin_mag = jnp.where(odd, cosine, sine)
    cos_val = jnp.where(((quarter + 1) & 2) == 2, -cos_mag, cos_mag)
    sin_val = jnp.where((quarter & 2) == 2, -sin_mag, sin_mag)
    return cos_val, sin_val


def lane_block(shape):
    return lax.broadcasted_iota(jnp.int32, shape, 1) >> 5


def slots_to_pairs(read_block, group):
    blocks = [read_block(4 * group + member) for member in range(4)]
    where = lane_block(blocks[0].shape)
    rows = []
    for turn in range(4):
        total = None
        for member in range(4):
            shift = 32 * (member - turn) % 128
            moved = pltpu.roll(blocks[member], shift, 1) if shift else blocks[member]
            total = moved if total is None else jnp.where(where == member, moved, total)
        rows.append(total)
    return rows


def pairs_to_slots(rows):
    where = lane_block(rows[0].shape)
    blocks = []
    for member in range(4):
        total = None
        for turn in range(4):
            shift = 32 * (turn - member) % 128
            moved = pltpu.roll(rows[turn], shift, 1) if shift else rows[turn]
            total = moved if total is None else jnp.where(where == turn, moved, total)
        blocks.append(total)
    return blocks


def wide_row(block):
    return jnp.concatenate([block[k : k + 1, :] for k in range(4)], axis=1)


def tall_block(row):
    return jnp.concatenate([row[:, 128 * k : 128 * (k + 1)] for k in range(4)], axis=0)


def jones_outer(left, right):
    real_rows = []
    imag_rows = []
    for row_a in range(2):
        for row_b in range(2):
            real_sum = 0.0
            imag_sum = 0.0
            for inner in range(2):
                left_re = left[row_a * 2 + inner]
                left_im = left[4 + row_a * 2 + inner]
                right_re = right[row_b * 2 + inner]
                right_im = right[4 + row_b * 2 + inner]
                real_sum = real_sum + left_re * right_re + left_im * right_im
                imag_sum = imag_sum + left_im * right_re - left_re * right_im
            real_rows.append(real_sum)
            imag_rows.append(imag_sum)
    return jnp.concatenate(real_rows, axis=0), jnp.concatenate(imag_rows, axis=0)


def jones_stokes(left, right, resid):
    total_re = 0.0
    total_im = 0.0
    for inner in range(2):
        for row_a in range(2):
            for row_b in range(2):
                left_re = left[row_a * 2 + inner]
                left_im = left[4 + row_a * 2 + inner]
                res_re = resid[row_a * 2 + row_b]
                res_im = resid[4 + row_a * 2 + row_b]
                right_re = right[row_b * 2 + inner]
                right_im = right[4 + row_b * 2 + inner]
                mid_re = left_re * res_re + left_im * res_im
                mid_im = left_re * res_im - left_im * res_re
                total_re = total_re + mid_re * right_re - mid_im * right_im
                total_im = total_im + mid_re * right_im + mid_im * right_re
    return 0.5 * total_re, 0.5 * total_im


def kernel(
    n_vis,
    n_facet,
    vis_ref,
    weight_ref,
    live_ref,
    station_p_ref,
    station_q_ref,
    interval_ref,
    cell_row_ref,
    cell_col_ref,
    gain_ref,
    image_ref,
    first_hi_ref,
    first_lo_ref,
    last_hi_ref,
    last_lo_ref,
    twist_ref,
    resid_ref,
    dirty_ref,
    gain_all,
    part_out,
    part_in,
    pred_in,
    stokes_in,
    lines,
    work_re,
    work_im,
    table,
    cells,
    values,
    block_cos,
    block_sin,
    fine_cos,
    fine_sin,
    gain_send,
    gain_recv,
    part_send,
    part_recv,
    pred_send,
    pred_recv,
    stokes_send,
    stokes_recv,
):
    me = lax.axis_index("vis")
    facet = lax.axis_index("facet")
    side_x = image_ref.shape[0]

    def vis_peer(step):
        return lax.rem(me + step, n_vis)

    def facet_peer(step):
        return lax.rem(facet + step, n_facet)

    barrier = pltpu.get_barrier_semaphore()

    def greet_vis(step, carry):
        pl.semaphore_signal(barrier, 1, device_id=(vis_peer(step), facet), device_id_type=MESH)
        return carry

    def greet_facet(step, carry):
        pl.semaphore_signal(barrier, 1, device_id=(me, facet_peer(step)), device_id_type=MESH)
        return carry

    lax.fori_loop(1, n_vis, greet_vis, 0)
    lax.fori_loop(1, n_facet, greet_facet, 0)

    def send_all(source, target, send_sem, recv_sem):
        def send(step, carry):
            pltpu.make_async_remote_copy(
                src_ref=source(vis_peer(step)),
                dst_ref=target.at[me],
                send_sem=send_sem,
                recv_sem=recv_sem,
                device_id=(vis_peer(step), facet),
                device_id_type=MESH,
            ).start()
            return carry

        lax.fori_loop(1, n_vis, send, 0)

    def wait_blocks(buffer, count, sem):
        view = buffer.at[pl.ds(0, count)]
        pltpu.make_async_copy(view, view, sem).wait()

    intervals_here = gain_ref.shape[1]
    stations = gain_ref.shape[2]
    gain_all[me] = jnp.zeros((8, 256), F32)
    for comp in range(8):
        half, lane = comp // 4, 64 * (comp % 4)
        gain_all[me, 4 * half : 4 * half + intervals_here, lane : lane + stations] = gain_ref[comp]

    pl.semaphore_wait(barrier, n_vis + n_facet - 2)
    send_all(lambda peer: gain_all.at[me], gain_all, gain_send, gain_recv)

    lines[...] = image_ref[...].T
    for b in range(RADIX):
        part = lines[pl.ds(b, INNER, stride=RADIX), :].T
        high, low = split_pair(part)
        both = matmul(high, first_hi_ref[...]) + (
            matmul(high, first_lo_ref[...]) + matmul(low, first_hi_ref[...])
        )
        re, im = both[:, :INNER], both[:, INNER:]
        cos = twist_ref[0, b : b + 1, :]
        sin = twist_ref[1, b : b + 1, :]
        work_re[b] = re * cos + im * sin
        work_im[b] = im * cos - re * sin

    def forward_rows(chunk, carry):
        rows = pl.ds(pl.multiple_of(chunk * 8, 8), 8)
        rows_im = pl.ds(pl.multiple_of(side_x + chunk * 8, 8), 8)
        vals = radix16([(work_re[b, rows, :], work_im[b, rows, :]) for b in range(RADIX)], -1.0)
        for q in range(RADIX):
            table[q, rows, :] = vals[q][0]
            table[q, rows_im, :] = vals[q][1]
        return carry

    lax.fori_loop(0, side_x // 8, forward_rows, 0)

    def order_cells(group, carry):
        lanes = pl.ds(pl.multiple_of(group * 128, 128), 128)

        def read(holder):
            rows = pl.ds(holder * 4, 4)
            return jnp.concatenate([cell_row_ref[rows, :], cell_col_ref[rows, :]], axis=0)

        for turn, rows in enumerate(slots_to_pairs(read, group)):
            cells[8 * turn : 8 * turn + 8, lanes] = rows
        return carry

    lax.fori_loop(0, n_vis // 4, order_cells, 0)

    width = cells.shape[1]
    chunk_w = 256

    def pair_row(pair):
        return lax.rem(pair, 4) * 8 + pair // 4

    def one_hot(pair, lanes):
        local = cells[pl.ds(pair_row(pair), 1), lanes]
        lane = lax.broadcasted_iota(jnp.int32, local.shape, 1)
        local = local + ((lane >> 4) & 1) * 64
        index = lax.broadcasted_iota(jnp.int32, (INNER, local.shape[1]), 0)
        return jnp.where(index == local, 1.0, 0.0).astype(BF16)

    def forward_pair(pair, carry):
        column = cells[pl.ds(pair_row(pair) + 4, 1), :]
        index = lax.broadcasted_iota(jnp.int32, (8, width), 0)
        cos, sin = unit_phase((column * (me * side_x + 8 * index)) & (SIDE - 1))
        block_cos[pair] = cos
        block_sin[pair] = sin
        cos, sin = unit_phase((column * index) & (SIDE - 1))
        fine_cos[pair] = cos
        fine_sin[pair] = sin
        high, low = split_pair(table[pair])
        both = jnp.concatenate([high, low], axis=0)
        for start in range(0, width, chunk_w):
            lanes = slice(start, start + chunk_w)
            picked = matmul(both, one_hot(pair, lanes))
            picked = picked[: 2 * side_x] + picked[2 * side_x :]
            sum_re = 0.0
            sum_im = 0.0
            for block in range(side_x // 8):
                re = picked[8 * block : 8 * block + 8]
                im = picked[side_x + 8 * block : side_x + 8 * block + 8]
                cos = block_cos[pair, block : block + 1, lanes]
                sin = block_sin[pair, block : block + 1, lanes]
                sum_re = sum_re + (re * cos + im * sin)
                sum_im = sum_im + (im * cos - re * sin)
            cos = fine_cos[pair, :, lanes]
            sin = fine_sin[pair, :, lanes]
            out_re = jnp.sum(sum_re * cos + sum_im * sin, axis=0, keepdims=True)
            out_im = jnp.sum(sum_im * cos - sum_re * sin, axis=0, keepdims=True)
            values[pl.ds(pair_row(pair), 1), lanes] = out_re
            values[pl.ds(pair_row(pair) + 4, 1), lanes] = out_im
        return carry

    lax.fori_loop(0, RADIX, forward_pair, 0)

    def pack_values(group, carry):
        lanes = pl.ds(pl.multiple_of(group * 128, 128), 128)
        rows = [values[8 * turn : 8 * turn + 8, lanes] for turn in range(4)]
        for member, block in enumerate(pairs_to_slots(rows)):
            part_out[4 * group + member] = block
        return carry

    lax.fori_loop(0, n_vis // 4, pack_values, 0)
    send_all(lambda peer: part_out.at[peer], part_in, part_send, part_recv)
    part_in[me] = part_out[me]

    wait_blocks(gain_all, n_vis - 1, gain_recv)
    high, low = split_pair(gain_all[...].reshape(n_vis * 8, 256).T)
    both = jnp.concatenate([high, low], axis=0)
    interval = wide_row(interval_ref[...])
    gain_row = (interval >> 2) * 8 + (interval & 3)
    station_p = wide_row(station_p_ref[...])
    station_q = wide_row(station_q_ref[...])
    slots = interval.shape[1]
    station = lax.broadcasted_iota(jnp.int32, (64, slots), 0)
    at_p = jnp.where(station == station_p, 1.0, 0.0)
    at_q = jnp.where(station == station_q, 1.0, 0.0)
    index = lax.broadcasted_iota(jnp.int32, (n_vis * 8, slots), 0)
    jones_p = []
    jones_q = []
    for half in range(2):
        hot = jnp.where(index == gain_row + 4 * half, 1.0, 0.0).astype(BF16)
        picked = matmul(both, hot)
        picked = picked[:256] + picked[256:]
        for comp in range(4):
            here = picked[64 * comp : 64 * comp + 64]
            jones_p.append(jnp.sum(here * at_p, axis=0, keepdims=True))
            jones_q.append(jnp.sum(here * at_q, axis=0, keepdims=True))
    outer_re, outer_im = jones_outer(jones_p, jones_q)
    live = wide_row(live_ref[...]).astype(F32)
    scale = wide_row(weight_ref[...]) * live

    wait_blocks(part_in, n_vis - 1, part_recv)
    model = jnp.sum(part_in[...], axis=0) * (1.0 / SIDE)
    model_re = wide_row(model[0:4])
    model_im = wide_row(model[4:8])
    pred_in[facet, 0:4, :] = model_re * outer_re - model_im * outer_im
    pred_in[facet, 4:8, :] = model_re * outer_im + model_im * outer_re

    def send_pred(step, carry):
        pltpu.make_async_remote_copy(
            src_ref=pred_in.at[facet],
            dst_ref=pred_in.at[facet],
            send_sem=pred_send,
            recv_sem=pred_recv,
            device_id=(me, facet_peer(step)),
            device_id_type=MESH,
        ).start()
        return carry

    lax.fori_loop(1, n_facet, send_pred, 0)
    wait_blocks(pred_in, n_facet - 1, pred_recv)
    predicted = pred_in[0]
    for other in range(1, n_facet):
        predicted = predicted + pred_in[other]
    resid = (vis_ref[...] - predicted) * live
    resid_ref[...] = resid
    stokes_re, stokes_im = jones_stokes(jones_p, jones_q, [resid[c : c + 1] for c in range(8)])
    stokes_in[me, 0:4, :] = tall_block(stokes_re * scale)
    stokes_in[me, 4:8, :] = tall_block(stokes_im * scale)
    send_all(lambda peer: stokes_in.at[me], stokes_in, stokes_send, stokes_recv)
    wait_blocks(stokes_in, n_vis - 1, stokes_recv)

    def order_stokes(group, carry):
        lanes = pl.ds(pl.multiple_of(group * 128, 128), 128)
        for turn, rows in enumerate(slots_to_pairs(lambda holder: stokes_in[holder], group)):
            values[8 * turn : 8 * turn + 8, lanes] = rows
        return carry

    lax.fori_loop(0, n_vis // 4, order_stokes, 0)

    def backward_pair(pair, carry):
        total = jnp.zeros((4 * side_x, INNER), F32)
        for start in range(0, width, chunk_w):
            lanes = slice(start, start + chunk_w)
            re = values[pl.ds(pair_row(pair), 1), lanes]
            im = values[pl.ds(pair_row(pair) + 4, 1), lanes]
            cos = fine_cos[pair, :, lanes]
            sin = fine_sin[pair, :, lanes]
            fine_re = re * cos - im * sin
            fine_im = re * sin + im * cos
            real_rows = []
            imag_rows = []
            for block in range(side_x // 8):
                cos = block_cos[pair, block : block + 1, lanes]
                sin = block_sin[pair, block : block + 1, lanes]
                real_rows.append(fine_re * cos - fine_im * sin)
                imag_rows.append(fine_re * sin + fine_im * cos)
            high, low = split_pair(jnp.concatenate(real_rows + imag_rows, axis=0))
            both = jnp.concatenate([high, low], axis=0)
            total = total + lax.dot_general(
                both,
                one_hot(pair, lanes),
                (((1,), (1,)), ((), ())),
                preferred_element_type=F32,
            )
        table[pair] = total[: 2 * side_x] + total[2 * side_x :]
        return carry

    lax.fori_loop(0, RADIX, backward_pair, 0)

    def backward_rows(chunk, carry):
        rows = pl.ds(pl.multiple_of(chunk * 8, 8), 8)
        rows_im = pl.ds(pl.multiple_of(side_x + chunk * 8, 8), 8)
        vals = radix16([(table[q, rows, :], table[q, rows_im, :]) for q in range(RADIX)], 1.0)
        for b in range(RADIX):
            re, im = vals[b]
            cos = twist_ref[0, b : b + 1, :]
            sin = twist_ref[1, b : b + 1, :]
            work_re[b, rows, :] = re * cos - im * sin
            work_im[b, rows, :] = re * sin + im * cos
        return carry

    lax.fori_loop(0, side_x // 8, backward_rows, 0)

    factor = 4.0 / math.sqrt(slots * n_vis)
    for b in range(RADIX):
        high, low = split_pair(jnp.concatenate([work_re[b], work_im[b]], axis=1))
        part = matmul(high, last_hi_ref[...]) + (
            matmul(high, last_lo_ref[...]) + matmul(low, last_hi_ref[...])
        )
        lines[pl.ds(b, INNER, stride=RADIX), :] = (part * factor).T
    dirty_ref[...] = lines[...].T

    wait_blocks(gain_all, n_vis - 1, gain_send)
    wait_blocks(part_in, n_vis - 1, part_send)
    wait_blocks(pred_in, n_facet - 1, pred_send)
    wait_blocks(stokes_in, n_vis - 1, stokes_send)


def per_device(
    visibilities,
    weights,
    live_slots,
    station_p,
    station_q,
    interval,
    cell_row,
    cell_col,
    jones_gains,
    model_image,
):
    n_vis = lax.axis_size("vis")
    n_facet = lax.axis_size("facet")
    side_x = model_image.shape[1]
    slots = visibilities.shape[1]
    width = n_vis * slots // RADIX

    def rows_of(array):
        return array.reshape(-1, 128)

    tables = [jnp.asarray(table) for table in make_tables()]
    vmem = pl.BlockSpec(memory_space=pltpu.VMEM)
    resid, dirty = pl.pallas_call(
        functools.partial(kernel, n_vis, n_facet),
        out_shape=(
            jax.ShapeDtypeStruct((8, slots), F32),
            jax.ShapeDtypeStruct((side_x, SIDE), F32),
        ),
        in_specs=[vmem] * 15,
        out_specs=(vmem, vmem),
        scratch_shapes=[
            pltpu.VMEM((n_vis, 8, 256), F32),
            pltpu.VMEM((n_vis, 8, 128), F32),
            pltpu.VMEM((n_vis, 8, 128), F32),
            pltpu.VMEM((n_facet, 8, slots), F32),
            pltpu.VMEM((n_vis, 8, 128), F32),
            pltpu.VMEM((SIDE, side_x), F32),
            pltpu.VMEM((RADIX, side_x, INNER), F32),
            pltpu.VMEM((RADIX, side_x, INNER), F32),
            pltpu.VMEM((RADIX, 2 * side_x, INNER), F32),
            pltpu.VMEM((32, width), jnp.int32),
            pltpu.VMEM((32, width), F32),
            pltpu.VMEM((RADIX, 8, width), F32),
            pltpu.VMEM((RADIX, 8, width), F32),
            pltpu.VMEM((RADIX, 8, width), F32),
            pltpu.VMEM((RADIX, 8, width), F32),
        ]
        + [pltpu.SemaphoreType.DMA(())] * 8,
        compiler_params=pltpu.CompilerParams(
            collective_id=0, has_side_effects=True, vmem_limit_bytes=40 * 1024 * 1024
        ),
    )(
        visibilities,
        rows_of(weights),
        rows_of(live_slots),
        rows_of(station_p),
        rows_of(station_q),
        rows_of(interval),
        rows_of(cell_row),
        rows_of(cell_col),
        jones_gains[0],
        model_image[0],
        *tables,
    )
    return resid, dirty[None]


def solution(mesh):
    return jax.shard_map(
        per_device,
        mesh=mesh,
        in_specs=(
            P(None, "vis"),
            P("vis"),
            P("vis"),
            P("vis"),
            P("vis"),
            P("vis"),
            P(),
            P(),
            P("facet", None, "vis", None),
            P("facet", "vis", None),
        ),
        out_specs=(P(None, "vis"), P("facet", "vis", None)),
        check_vma=False,
    )
```

```python
import functools
import math

import jax
import jax.numpy as jnp
import numpy as np
from jax import lax
from jax.experimental import pallas as pl
from jax.experimental.pallas import tpu as pltpu
from jax.sharding import PartitionSpec as P

TWO_PI = 2.0 * math.pi
MESH = pl.DeviceIdType.MESH
F32 = jnp.float32
BF16 = jnp.bfloat16

RADIX = 16
INNER = 128
SIDE = RADIX * INNER


def split_table(table):
    high = table.astype(BF16)
    low = (table - high.astype(np.float64)).astype(BF16)
    return high, low


def make_tables():
    inner = np.arange(INNER)
    angle = TWO_PI * (np.outer(inner, inner) % INNER) / INNER
    turn = np.concatenate([np.cos(angle), -np.sin(angle)], axis=0)
    twist = TWO_PI * np.outer(np.arange(RADIX), inner) / SIDE
    twist = np.stack([np.cos(twist), np.sin(twist)]).astype(np.float32)
    return np.concatenate(split_table(turn), axis=0), twist


def split_pair(value):
    high = value.astype(BF16)
    low = (value - high.astype(F32)).astype(BF16)
    return high, low


def matmul(left, right):
    return jnp.dot(left, right, preferred_element_type=F32)


def cmul_const(pair, real, imag):
    re, im = pair
    return re * real - im * imag, re * imag + im * real


def radix4(vals, sign):
    (ar, ai), (br, bi), (cr, ci), (dr, di) = vals
    sr, si = ar + cr, ai + ci
    tr, ti = ar - cr, ai - ci
    ur, ui = br + dr, bi + di
    wr, wi = br - dr, bi - di
    if sign < 0:
        xr, xi = wi, -wr
    else:
        xr, xi = -wi, wr
    return [(sr + ur, si + ui), (tr + xr, ti + xi), (sr - ur, si - ui), (tr - xr, ti - xi)]


def radix16(vals, sign):
    inner = [radix4([vals[4 * n1 + n2] for n1 in range(4)], sign) for n2 in range(4)]
    out = [None] * 16
    for k1 in range(4):
        column = []
        for n2 in range(4):
            turn = n2 * k1
            value = inner[n2][k1]
            if turn == 4:
                re, im = value
                value = (im, -re) if sign < 0 else (-im, re)
            elif turn == 2 or turn == 6:
                half = math.sqrt(0.5)
                re, im = value
                if sign < 0:
                    value = ((re + im) * half, (im - re) * half)
                else:
                    value = ((re - im) * half, (re + im) * half)
                if turn == 6:
                    re, im = value
                    value = (im, -re) if sign < 0 else (-im, re)
            elif turn:
                angle = sign * TWO_PI * turn / 16
                value = cmul_const(value, math.cos(angle), math.sin(angle))
            column.append(value)
        for k2, value in enumerate(radix4(column, sign)):
            out[k1 + 4 * k2] = value
    return out


def unit_phase(step):
    quarter = (step + 256) >> 9
    angle = (step - (quarter << 9)).astype(F32) * (TWO_PI / SIDE)
    square = angle * angle
    sine = angle * (
        1.0
        + square
        * (-1.0 / 6 + square * (1.0 / 120 + square * (-1.0 / 5040 + square * (1.0 / 362880))))
    )
    cosine = 1.0 + square * (
        -0.5 + square * (1.0 / 24 + square * (-1.0 / 720 + square * (1.0 / 40320)))
    )
    odd = (quarter & 1) == 1
    cos_mag = jnp.where(odd, sine, cosine)
    sin_mag = jnp.where(odd, cosine, sine)
    cos_val = jnp.where(((quarter + 1) & 2) == 2, -cos_mag, cos_mag)
    sin_val = jnp.where((quarter & 2) == 2, -sin_mag, sin_mag)
    return cos_val, sin_val


def lane_block(shape):
    return lax.broadcasted_iota(jnp.int32, shape, 1) >> 5


def slots_to_pairs(blocks):
    where = lane_block(blocks[0].shape)
    rows = []
    for turn in range(4):
        total = None
        for member in range(4):
            shift = 32 * (member - turn) % 128
            moved = pltpu.roll(blocks[member], shift, 1) if shift else blocks[member]
            total = moved if total is None else jnp.where(where == member, moved, total)
        rows.append(total)
    return rows


def pairs_to_slots(rows):
    where = lane_block(rows[0].shape)
    blocks = []
    for member in range(4):
        total = None
        for turn in range(4):
            shift = 32 * (turn - member) % 128
            moved = pltpu.roll(rows[turn], shift, 1) if shift else rows[turn]
            total = moved if total is None else jnp.where(where == turn, moved, total)
        blocks.append(total)
    return blocks


def wide_row(block):
    return jnp.concatenate([block[k : k + 1, :] for k in range(block.shape[0])], axis=1)


def tall_block(row):
    count = row.shape[1] // 128
    return jnp.concatenate([row[:, 128 * k : 128 * (k + 1)] for k in range(count)], axis=0)


def jones_outer(left, right):
    real_rows = []
    imag_rows = []
    for row_a in range(2):
        for row_b in range(2):
            real_sum = 0.0
            imag_sum = 0.0
            for inner in range(2):
                left_re = left[row_a * 2 + inner]
                left_im = left[4 + row_a * 2 + inner]
                right_re = right[row_b * 2 + inner]
                right_im = right[4 + row_b * 2 + inner]
                real_sum = real_sum + left_re * right_re + left_im * right_im
                imag_sum = imag_sum + left_im * right_re - left_re * right_im
            real_rows.append(real_sum)
            imag_rows.append(imag_sum)
    return jnp.concatenate(real_rows, axis=0), jnp.concatenate(imag_rows, axis=0)


def jones_stokes(left, right, resid):
    total_re = 0.0
    total_im = 0.0
    for inner in range(2):
        for row_a in range(2):
            for row_b in range(2):
                left_re = left[row_a * 2 + inner]
                left_im = left[4 + row_a * 2 + inner]
                res_re = resid[row_a * 2 + row_b]
                res_im = resid[4 + row_a * 2 + row_b]
                right_re = right[row_b * 2 + inner]
                right_im = right[4 + row_b * 2 + inner]
                mid_re = left_re * res_re + left_im * res_im
                mid_im = left_re * res_im - left_im * res_re
                total_re = total_re + mid_re * right_re - mid_im * right_im
                total_im = total_im + mid_re * right_im + mid_im * right_re
    return 0.5 * total_re, 0.5 * total_im


def exchange_kernel(
    n_vis,
    n_facet,
    vis_hbm,
    weight_hbm,
    live_hbm,
    station_p_hbm,
    station_q_hbm,
    interval_hbm,
    cell_row_hbm,
    cell_col_hbm,
    gain_hbm,
    image_hbm,
    turn_hbm,
    twist_hbm,
    resid_ref,
    table,
    turn_ref,
    twist_ref,
    vis_ref,
    weight_ref,
    live_ref,
    station_p_ref,
    station_q_ref,
    interval_ref,
    cell_row_ref,
    cell_col_ref,
    gain_ref,
    image_ref,
    gain_all,
    part_out,
    part_in,
    pred_in,
    stokes_in,
    lines,
    work_re,
    work_im,
    local_row,
    local_col,
    values,
    step_cos,
    step_sin,
    fine_cos,
    fine_sin,
    load_sem,
    gain_send,
    gain_recv,
    part_send,
    part_recv,
    pred_send,
    pred_recv,
    stokes_send,
    stokes_recv,
):
    me = lax.axis_index("vis")
    facet = lax.axis_index("facet")
    side_x = image_ref.shape[0]
    width = values.shape[2]
    slots = vis_ref.shape[1]
    part = slots // 2

    order = (
        (cell_row_hbm, cell_row_ref),
        (cell_col_hbm, cell_col_ref),
        (gain_hbm, gain_ref),
        (image_hbm, image_ref),
        (turn_hbm, turn_ref),
        (twist_hbm, twist_ref),
        (interval_hbm, interval_ref),
        (station_p_hbm, station_p_ref),
        (station_q_hbm, station_q_ref),
        (live_hbm, live_ref),
        (weight_hbm, weight_ref),
        (vis_hbm, vis_ref),
    )
    loads = [
        pltpu.make_async_copy(source, target, load_sem.at[place])
        for place, (source, target) in enumerate(order)
    ]
    for load in loads:
        load.start()

    def vis_peer(step):
        return lax.rem(me + step, n_vis)

    def facet_peer(step):
        return lax.rem(facet + step, n_facet)

    barrier = pltpu.get_barrier_semaphore()

    def greet_vis(step, carry):
        pl.semaphore_signal(barrier, 1, device_id=(vis_peer(step), facet), device_id_type=MESH)
        return carry

    def greet_facet(step, carry):
        pl.semaphore_signal(barrier, 1, device_id=(me, facet_peer(step)), device_id_type=MESH)
        return carry

    lax.fori_loop(1, n_vis, greet_vis, 0)
    lax.fori_loop(1, n_facet, greet_facet, 0)

    def send_all(source, target, send_sem, recv_sem):
        def send(step, carry):
            pltpu.make_async_remote_copy(
                src_ref=source(vis_peer(step)),
                dst_ref=target.at[me],
                send_sem=send_sem,
                recv_sem=recv_sem,
                device_id=(vis_peer(step), facet),
                device_id_type=MESH,
            ).start()
            return carry

        lax.fori_loop(1, n_vis, send, 0)

    def wait_blocks(buffer, count, sem):
        view = buffer.at[pl.ds(0, count)]
        pltpu.make_async_copy(view, view, sem).wait()

    def pair_row(pair):
        return lax.rem(pair, 4) * 4 + pair // 4

    loads[0].wait()
    loads[1].wait()

    def order_cells(group, carry):
        lanes = pl.ds(pl.multiple_of(group * 128, 128), 128)

        def read(holder):
            rows = pl.ds(holder * 4, 4)
            return jnp.concatenate([cell_row_ref[rows, :], cell_col_ref[rows, :]], axis=0)

        for turn, rows in enumerate(slots_to_pairs([read(4 * group + k) for k in range(4)])):
            lane = lax.broadcasted_iota(jnp.int32, (4, 128), 1)
            local_row[4 * turn : 4 * turn + 4, lanes] = rows[0:4] + ((lane >> 4) & 1) * 64
            local_col[4 * turn : 4 * turn + 4, lanes] = rows[4:8]
        return carry

    lax.fori_loop(0, n_vis // 4, order_cells, 0)
    cos, sin = unit_phase((local_col[...] * 8) & (SIDE - 1))
    step_cos[...] = cos
    step_sin[...] = sin

    def fine_phases(pair, carry):
        column = local_col[pl.ds(pair_row(pair), 1), :]
        index = lax.broadcasted_iota(jnp.int32, (8, width), 0)
        cos, sin = unit_phase((column * (me * side_x + index)) & (SIDE - 1))
        fine_cos[pair] = cos
        fine_sin[pair] = sin
        return carry

    lax.fori_loop(0, RADIX, fine_phases, 0)

    loads[2].wait()
    intervals_here = gain_ref.shape[1]
    stations = gain_ref.shape[2]
    gain_all[me] = jnp.zeros((8, 256), F32)
    for comp in range(8):
        half, lane = comp // 4, 64 * (comp % 4)
        gain_all[me, 4 * half : 4 * half + intervals_here, lane : lane + stations] = gain_ref[comp]

    pl.semaphore_wait(barrier, n_vis + n_facet - 2)
    send_all(lambda peer: gain_all.at[me], gain_all, gain_send, gain_recv)

    loads[3].wait()
    lines[...] = image_ref[...].T
    loads[4].wait()
    loads[5].wait()
    first_hi = jnp.concatenate([turn_ref[:INNER], turn_ref[INNER : 2 * INNER]], axis=1)
    first_lo = jnp.concatenate([turn_ref[2 * INNER : 3 * INNER], turn_ref[3 * INNER :]], axis=1)
    for b in range(RADIX):
        high, low = split_pair(lines[pl.ds(b, INNER, stride=RADIX), :].T)
        both = matmul(high, first_hi) + (matmul(high, first_lo) + matmul(low, first_hi))
        re, im = both[:, :INNER], both[:, INNER:]
        cos = twist_ref[0, b : b + 1, :]
        sin = twist_ref[1, b : b + 1, :]
        work_re[b] = re * cos + im * sin
        work_im[b] = im * cos - re * sin

    def forward_rows(chunk, carry):
        rows = pl.ds(pl.multiple_of(chunk * 8, 8), 8)
        rows_im = pl.ds(pl.multiple_of(side_x + chunk * 8, 8), 8)
        vals = radix16([(work_re[b, rows, :], work_im[b, rows, :]) for b in range(RADIX)], -1.0)
        for q in range(RADIX):
            table[q, rows, :] = vals[q][0]
            table[q, rows_im, :] = vals[q][1]
        return carry

    lax.fori_loop(0, side_x // 8, forward_rows, 0)

    chunk_w = 256
    blocks_x = side_x // 8

    def one_hot(pair, lanes):
        local = local_row[pl.ds(pair_row(pair), 1), lanes]
        index = lax.broadcasted_iota(jnp.int32, (INNER, local.shape[1]), 0)
        return jnp.where(index == local, 1.0, 0.0).astype(BF16)

    def value_row(pair):
        return lax.rem(pair, 4) * 4 + lax.rem(pair // 4, 2)

    def forward_pair(pair, carry):
        high, low = split_pair(table[pair])
        both = jnp.concatenate([high, low], axis=0)
        half = pair // 8
        for start in range(0, width, chunk_w):
            lanes = slice(start, start + chunk_w)
            picked = matmul(both, one_hot(pair, lanes))
            picked = picked[: 2 * side_x] + picked[2 * side_x :]
            cos = step_cos[pl.ds(pair_row(pair), 1), lanes]
            sin = step_sin[pl.ds(pair_row(pair), 1), lanes]
            last = 8 * (blocks_x - 1)
            sum_re = picked[last : last + 8]
            sum_im = picked[side_x + last : side_x + last + 8]
            for block in range(blocks_x - 2, -1, -1):
                re = picked[8 * block : 8 * block + 8]
                im = picked[side_x + 8 * block : side_x + 8 * block + 8]
                sum_re, sum_im = (
                    re + (sum_re * cos + sum_im * sin),
                    im + (sum_im * cos - sum_re * sin),
                )
            cos = fine_cos[pair, :, lanes]
            sin = fine_sin[pair, :, lanes]
            out_re = jnp.sum(sum_re * cos + sum_im * sin, axis=0, keepdims=True)
            out_im = jnp.sum(sum_im * cos - sum_re * sin, axis=0, keepdims=True)
            values[half, pl.ds(value_row(pair), 1), lanes] = out_re
            values[half, pl.ds(value_row(pair) + 2, 1), lanes] = out_im
        return carry

    for half in range(2):
        lax.fori_loop(8 * half, 8 * half + 8, forward_pair, 0)

        def pack_values(group, carry):
            lanes = pl.ds(pl.multiple_of(group * 128, 128), 128)
            rows = [values[half, 4 * turn : 4 * turn + 4, lanes] for turn in range(4)]
            for member, block in enumerate(pairs_to_slots(rows)):
                part_out[half, 4 * group + member] = block
            return carry

        lax.fori_loop(0, n_vis // 4, pack_values, 0)
        send_all(
            lambda peer: part_out.at[half, peer],
            part_in.at[half],
            part_send.at[half],
            part_recv.at[half],
        )
        part_in[half, me] = part_out[half, me]

    for load in loads[6:]:
        load.wait()
    wait_blocks(gain_all, n_vis - 1, gain_recv)
    high, low = split_pair(gain_all[...].reshape(n_vis * 8, 256).T)
    both = jnp.concatenate([high, low], axis=0)
    interval = wide_row(interval_ref[...])
    gain_row = (interval >> 2) * 8 + (interval & 3)
    station = lax.broadcasted_iota(jnp.int32, (64, slots), 0)
    at_p = jnp.where(station == wide_row(station_p_ref[...]), 1.0, 0.0)
    at_q = jnp.where(station == wide_row(station_q_ref[...]), 1.0, 0.0)
    index = lax.broadcasted_iota(jnp.int32, (n_vis * 8, slots), 0)
    jones_p = []
    jones_q = []
    for half in range(2):
        hot = jnp.where(index == gain_row + 4 * half, 1.0, 0.0).astype(BF16)
        picked = matmul(both, hot)
        picked = picked[:256] + picked[256:]
        for comp in range(4):
            here = picked[64 * comp : 64 * comp + 64]
            jones_p.append(jnp.sum(here * at_p, axis=0, keepdims=True))
            jones_q.append(jnp.sum(here * at_q, axis=0, keepdims=True))
    outer_re, outer_im = jones_outer(jones_p, jones_q)
    live = wide_row(live_ref[...]).astype(F32)
    scale = wide_row(weight_ref[...]) * live

    for half in range(2):
        here = slice(half * part, (half + 1) * part)
        wait_blocks(part_in.at[half], n_vis - 1, part_recv.at[half])
        model = jnp.sum(part_in[half], axis=0) * (1.0 / SIDE)
        model_re = wide_row(model[0:2])
        model_im = wide_row(model[2:4])
        own_re, own_im = outer_re[:, here], outer_im[:, here]
        pred_in[half, facet, 0:4, :] = model_re * own_re - model_im * own_im
        pred_in[half, facet, 4:8, :] = model_re * own_im + model_im * own_re

        def send_pred(step, carry):
            pltpu.make_async_remote_copy(
                src_ref=pred_in.at[half, facet],
                dst_ref=pred_in.at[half, facet],
                send_sem=pred_send.at[half],
                recv_sem=pred_recv.at[half],
                device_id=(me, facet_peer(step)),
                device_id_type=MESH,
            ).start()
            return carry

        lax.fori_loop(1, n_facet, send_pred, 0)

    for half in range(2):
        here = slice(half * part, (half + 1) * part)
        wait_blocks(pred_in.at[half], n_facet - 1, pred_recv.at[half])
        predicted = pred_in[half, 0]
        for other in range(1, n_facet):
            predicted = predicted + pred_in[half, other]
        resid = (vis_ref[:, here] - predicted) * live[:, here]
        resid_ref[:, here] = resid
        stokes_re, stokes_im = jones_stokes(
            [gain[:, here] for gain in jones_p],
            [gain[:, here] for gain in jones_q],
            [resid[comp : comp + 1] for comp in range(8)],
        )
        stokes_in[half, me, 0:2, :] = tall_block(stokes_re * scale[:, here])
        stokes_in[half, me, 2:4, :] = tall_block(stokes_im * scale[:, here])
        send_all(
            lambda peer: stokes_in.at[half, me],
            stokes_in.at[half],
            stokes_send.at[half],
            stokes_recv.at[half],
        )

    def backward_pair(pair, carry):
        total = jnp.zeros((4 * side_x, INNER), F32)
        half = pair // 8
        for start in range(0, width, chunk_w):
            lanes = slice(start, start + chunk_w)
            re = values[half, pl.ds(value_row(pair), 1), lanes]
            im = values[half, pl.ds(value_row(pair) + 2, 1), lanes]
            cos = fine_cos[pair, :, lanes]
            sin = fine_sin[pair, :, lanes]
            real_rows = [re * cos - im * sin]
            imag_rows = [re * sin + im * cos]
            cos = step_cos[pl.ds(pair_row(pair), 1), lanes]
            sin = step_sin[pl.ds(pair_row(pair), 1), lanes]
            for _ in range(blocks_x - 1):
                re, im = real_rows[-1], imag_rows[-1]
                real_rows.append(re * cos - im * sin)
                imag_rows.append(re * sin + im * cos)
            high, low = split_pair(jnp.concatenate(real_rows + imag_rows, axis=0))
            both = jnp.concatenate([high, low], axis=0)
            total = total + lax.dot_general(
                both,
                one_hot(pair, lanes),
                (((1,), (1,)), ((), ())),
                preferred_element_type=F32,
            )
        table[pair] = total[: 2 * side_x] + total[2 * side_x :]
        return carry

    for half in range(2):
        wait_blocks(stokes_in.at[half], n_vis - 1, stokes_recv.at[half])

        def order_stokes(group, carry):
            lanes = pl.ds(pl.multiple_of(group * 128, 128), 128)
            blocks = [stokes_in[half, 4 * group + member] for member in range(4)]
            for turn, rows in enumerate(slots_to_pairs(blocks)):
                values[half, 4 * turn : 4 * turn + 4, lanes] = rows
            return carry

        lax.fori_loop(0, n_vis // 4, order_stokes, 0)
        lax.fori_loop(8 * half, 8 * half + 8, backward_pair, 0)

    wait_blocks(gain_all, n_vis - 1, gain_send)
    for half in range(2):
        wait_blocks(part_in.at[half], n_vis - 1, part_send.at[half])
        wait_blocks(pred_in.at[half], n_facet - 1, pred_send.at[half])
        wait_blocks(stokes_in.at[half], n_vis - 1, stokes_send.at[half])


def image_kernel(
    factor,
    resid_ref,
    table,
    turn_ref,
    twist_ref,
    resid_hbm,
    dirty_hbm,
    work_re,
    work_im,
    lines,
    dirty,
    resid_sem,
    dirty_sem,
):
    side_x = dirty.shape[0]
    keep = pltpu.make_async_copy(resid_ref, resid_hbm, resid_sem)
    keep.start()

    def backward_rows(chunk, carry):
        rows = pl.ds(pl.multiple_of(chunk * 8, 8), 8)
        rows_im = pl.ds(pl.multiple_of(side_x + chunk * 8, 8), 8)
        vals = radix16([(table[q, rows, :], table[q, rows_im, :]) for q in range(RADIX)], 1.0)
        for b in range(RADIX):
            re, im = vals[b]
            cos = twist_ref[0, b : b + 1, :]
            sin = twist_ref[1, b : b + 1, :]
            work_re[b, rows, :] = re * cos - im * sin
            work_im[b, rows, :] = re * sin + im * cos
        return carry

    lax.fori_loop(0, side_x // 8, backward_rows, 0)

    last_hi = turn_ref[: 2 * INNER]
    last_lo = turn_ref[2 * INNER :]
    for b in range(RADIX):
        high, low = split_pair(jnp.concatenate([work_re[b], work_im[b]], axis=1))
        part = matmul(high, last_hi) + (matmul(high, last_lo) + matmul(low, last_hi))
        lines[pl.ds(b, INNER, stride=RADIX), :] = (part * factor).T
    count = dirty_sem.shape[0]
    wide = SIDE // count
    copies = []
    for piece in range(count):
        here = slice(piece * wide, (piece + 1) * wide)
        dirty[:, here] = lines[here, :].T
        copies.append(
            pltpu.make_async_copy(dirty.at[:, here], dirty_hbm.at[:, here], dirty_sem.at[piece])
        )
        copies[-1].start()
    for copy in copies:
        copy.wait()
    keep.wait()


def per_device(
    visibilities,
    weights,
    live_slots,
    station_p,
    station_q,
    interval,
    cell_row,
    cell_col,
    jones_gains,
    model_image,
):
    n_vis = lax.axis_size("vis")
    n_facet = lax.axis_size("facet")
    side_x = model_image.shape[1]
    slots = visibilities.shape[1]
    width = n_vis * slots // RADIX

    def rows_of(array):
        return array.reshape(-1, 128)

    turn, twist = [jnp.asarray(table) for table in make_tables()]
    given = [
        visibilities,
        rows_of(weights),
        rows_of(live_slots),
        rows_of(station_p),
        rows_of(station_q),
        rows_of(interval),
        rows_of(cell_row),
        rows_of(cell_col),
        jones_gains[0],
        model_image[0],
        turn,
        twist,
    ]
    in_hbm = pl.BlockSpec(memory_space=pltpu.HBM)
    in_vmem = pl.BlockSpec(memory_space=pltpu.VMEM)
    work = pltpu.VMEM((RADIX, side_x, INNER), F32)
    kept = pl.pallas_call(
        functools.partial(exchange_kernel, n_vis, n_facet),
        out_shape=(
            pltpu.VMEM((8, slots), F32),
            pltpu.VMEM((RADIX, 2 * side_x, INNER), F32),
            pltpu.VMEM(turn.shape, turn.dtype),
            pltpu.VMEM(twist.shape, twist.dtype),
        ),
        in_specs=[in_hbm] * len(given),
        out_specs=(in_vmem,) * 4,
        scratch_shapes=[pltpu.VMEM(array.shape, array.dtype) for array in given[:-2]]
        + [
            pltpu.VMEM((n_vis, 8, 256), F32),
            pltpu.VMEM((2, n_vis, 4, 128), F32),
            pltpu.VMEM((2, n_vis, 4, 128), F32),
            pltpu.VMEM((2, n_facet, 8, slots // 2), F32),
            pltpu.VMEM((2, n_vis, 4, 128), F32),
            pltpu.VMEM((SIDE, side_x), F32),
            work,
            work,
            pltpu.VMEM((16, width), jnp.int32),
            pltpu.VMEM((16, width), jnp.int32),
            pltpu.VMEM((2, 16, width), F32),
            pltpu.VMEM((16, width), F32),
            pltpu.VMEM((16, width), F32),
            pltpu.VMEM((RADIX, 8, width), F32),
            pltpu.VMEM((RADIX, 8, width), F32),
            pltpu.SemaphoreType.DMA((len(given),)),
            pltpu.SemaphoreType.DMA(()),
            pltpu.SemaphoreType.DMA(()),
        ]
        + [pltpu.SemaphoreType.DMA((2,))] * 6,
        compiler_params=pltpu.CompilerParams(
            collective_id=0, has_side_effects=True, vmem_limit_bytes=40 * 1024 * 1024
        ),
    )(*[pltpu.with_memory_space_constraint(array, pltpu.HBM) for array in given])
    resid, dirty = pl.pallas_call(
        functools.partial(image_kernel, 4.0 / math.sqrt(slots * n_vis)),
        out_shape=(
            pltpu.HBM((8, slots), F32),
            pltpu.HBM((side_x, SIDE), F32),
        ),
        in_specs=[in_vmem] * 4,
        out_specs=(in_hbm, in_hbm),
        scratch_shapes=[
            work,
            work,
            pltpu.VMEM((SIDE, side_x), F32),
            pltpu.VMEM((side_x, SIDE), F32),
            pltpu.SemaphoreType.DMA(()),
            pltpu.SemaphoreType.DMA((4,)),
        ],
        compiler_params=pltpu.CompilerParams(vmem_limit_bytes=40 * 1024 * 1024),
    )(*kept)
    return resid, dirty[None]


def solution(mesh):
    return jax.shard_map(
        per_device,
        mesh=mesh,
        in_specs=(
            P(None, "vis"),
            P("vis"),
            P("vis"),
            P("vis"),
            P("vis"),
            P("vis"),
            P(),
            P(),
            P("facet", None, "vis", None),
            P("facet", "vis", None),
        ),
        out_specs=(P(None, "vis"), P("facet", "vis", None)),
        check_vma=False,
    )
```

```python
import functools
import math

import jax
import jax.numpy as jnp
import numpy as np
from jax import lax
from jax.experimental import pallas as pl
from jax.experimental.pallas import tpu as pltpu
from jax.sharding import PartitionSpec as P

TWO_PI = 2.0 * math.pi
MESH = pl.DeviceIdType.MESH
F32 = jnp.float32
BF16 = jnp.bfloat16

RADIX = 16
INNER = 128
SIDE = RADIX * INNER


def split_table(table):
    high = table.astype(BF16)
    low = (table - high.astype(np.float64)).astype(BF16)
    return high, low


def make_tables():
    inner = np.arange(INNER)
    angle = TWO_PI * (np.outer(inner, inner) % INNER) / INNER
    turn = np.concatenate([np.cos(angle), -np.sin(angle)], axis=0)
    twist = TWO_PI * np.outer(np.arange(RADIX), inner) / SIDE
    twist = np.stack([np.cos(twist), np.sin(twist)]).astype(np.float32)
    return np.concatenate(split_table(turn), axis=0), twist


def split_pair(value):
    high = value.astype(BF16)
    low = (value - high.astype(F32)).astype(BF16)
    return high, low


def matmul(left, right):
    return jnp.dot(left, right, preferred_element_type=F32)


def cmul_const(pair, real, imag):
    re, im = pair
    return re * real - im * imag, re * imag + im * real


def radix4(vals, sign):
    (ar, ai), (br, bi), (cr, ci), (dr, di) = vals
    sr, si = ar + cr, ai + ci
    tr, ti = ar - cr, ai - ci
    ur, ui = br + dr, bi + di
    wr, wi = br - dr, bi - di
    if sign < 0:
        xr, xi = wi, -wr
    else:
        xr, xi = -wi, wr
    return [(sr + ur, si + ui), (tr + xr, ti + xi), (sr - ur, si - ui), (tr - xr, ti - xi)]


def radix16(vals, sign):
    inner = [radix4([vals[4 * n1 + n2] for n1 in range(4)], sign) for n2 in range(4)]
    out = [None] * 16
    for k1 in range(4):
        column = []
        for n2 in range(4):
            turn = n2 * k1
            value = inner[n2][k1]
            if turn == 4:
                re, im = value
                value = (im, -re) if sign < 0 else (-im, re)
            elif turn == 2 or turn == 6:
                half = math.sqrt(0.5)
                re, im = value
                if sign < 0:
                    value = ((re + im) * half, (im - re) * half)
                else:
                    value = ((re - im) * half, (re + im) * half)
                if turn == 6:
                    re, im = value
                    value = (im, -re) if sign < 0 else (-im, re)
            elif turn:
                angle = sign * TWO_PI * turn / 16
                value = cmul_const(value, math.cos(angle), math.sin(angle))
            column.append(value)
        for k2, value in enumerate(radix4(column, sign)):
            out[k1 + 4 * k2] = value
    return out


def unit_phase(step):
    quarter = (step + 256) >> 9
    angle = (step - (quarter << 9)).astype(F32) * (TWO_PI / SIDE)
    square = angle * angle
    sine = angle * (
        1.0
        + square
        * (-1.0 / 6 + square * (1.0 / 120 + square * (-1.0 / 5040 + square * (1.0 / 362880))))
    )
    cosine = 1.0 + square * (
        -0.5 + square * (1.0 / 24 + square * (-1.0 / 720 + square * (1.0 / 40320)))
    )
    odd = (quarter & 1) == 1
    cos_mag = jnp.where(odd, sine, cosine)
    sin_mag = jnp.where(odd, cosine, sine)
    cos_val = jnp.where(((quarter + 1) & 2) == 2, -cos_mag, cos_mag)
    sin_val = jnp.where((quarter & 2) == 2, -sin_mag, sin_mag)
    return cos_val, sin_val


def pick_lanes(value, index):
    numbers = lax.GatherDimensionNumbers(
        offset_dims=(),
        collapsed_slice_dims=(1,),
        start_index_map=(1,),
        operand_batching_dims=(0,),
        start_indices_batching_dims=(0,),
    )
    return lax.gather(
        value,
        index[..., None],
        numbers,
        slice_sizes=(1, 1),
        mode=lax.GatherScatterMode.PROMISE_IN_BOUNDS,
    )


def lane_block(shape):
    return lax.broadcasted_iota(jnp.int32, shape, 1) >> 5


def slots_to_pairs(blocks):
    where = lane_block(blocks[0].shape)
    rows = []
    for turn in range(4):
        total = None
        for member in range(4):
            shift = 32 * (member - turn) % 128
            moved = pltpu.roll(blocks[member], shift, 1) if shift else blocks[member]
            total = moved if total is None else jnp.where(where == member, moved, total)
        rows.append(total)
    return rows


def pairs_to_slots(rows):
    where = lane_block(rows[0].shape)
    blocks = []
    for member in range(4):
        total = None
        for turn in range(4):
            shift = 32 * (turn - member) % 128
            moved = pltpu.roll(rows[turn], shift, 1) if shift else rows[turn]
            total = moved if total is None else jnp.where(where == turn, moved, total)
        blocks.append(total)
    return blocks


def wide_row(block):
    return jnp.concatenate([block[k : k + 1, :] for k in range(block.shape[0])], axis=1)


def tall_block(row):
    count = row.shape[1] // 128
    return jnp.concatenate([row[:, 128 * k : 128 * (k + 1)] for k in range(count)], axis=0)


def jones_outer(left, right):
    real_rows = []
    imag_rows = []
    for row_a in range(2):
        for row_b in range(2):
            real_sum = 0.0
            imag_sum = 0.0
            for inner in range(2):
                left_re = left[row_a * 2 + inner]
                left_im = left[4 + row_a * 2 + inner]
                right_re = right[row_b * 2 + inner]
                right_im = right[4 + row_b * 2 + inner]
                real_sum = real_sum + left_re * right_re + left_im * right_im
                imag_sum = imag_sum + left_im * right_re - left_re * right_im
            real_rows.append(real_sum)
            imag_rows.append(imag_sum)
    return jnp.concatenate(real_rows, axis=0), jnp.concatenate(imag_rows, axis=0)


def jones_stokes(left, right, resid):
    total_re = 0.0
    total_im = 0.0
    for inner in range(2):
        for row_a in range(2):
            for row_b in range(2):
                left_re = left[row_a * 2 + inner]
                left_im = left[4 + row_a * 2 + inner]
                res_re = resid[row_a * 2 + row_b]
                res_im = resid[4 + row_a * 2 + row_b]
                right_re = right[row_b * 2 + inner]
                right_im = right[4 + row_b * 2 + inner]
                mid_re = left_re * res_re + left_im * res_im
                mid_im = left_re * res_im - left_im * res_re
                total_re = total_re + mid_re * right_re - mid_im * right_im
                total_im = total_im + mid_re * right_im + mid_im * right_re
    return 0.5 * total_re, 0.5 * total_im


def exchange_kernel(
    n_vis,
    n_facet,
    vis_hbm,
    weight_hbm,
    live_hbm,
    station_p_hbm,
    station_q_hbm,
    interval_hbm,
    cell_row_hbm,
    cell_col_hbm,
    gain_hbm,
    image_hbm,
    turn_hbm,
    twist_hbm,
    resid_ref,
    table,
    turn_ref,
    twist_ref,
    vis_ref,
    weight_ref,
    live_ref,
    station_p_ref,
    station_q_ref,
    interval_ref,
    cell_row_ref,
    cell_col_ref,
    gain_ref,
    image_ref,
    gain_all,
    part_out,
    part_in,
    pred_in,
    stokes_in,
    lines,
    work_re,
    work_im,
    local_row,
    local_col,
    values,
    step_cos,
    step_sin,
    fine_cos,
    fine_sin,
    load_sem,
    gain_send,
    gain_recv,
    part_send,
    part_recv,
    pred_send,
    pred_recv,
    stokes_send,
    stokes_recv,
):
    me = lax.axis_index("vis")
    facet = lax.axis_index("facet")
    side_x = image_ref.shape[0]
    width = values.shape[3]
    slots = vis_ref.shape[1]
    part = slots // 2

    order = (
        (cell_row_hbm, cell_row_ref),
        (cell_col_hbm, cell_col_ref),
        (gain_hbm, gain_ref),
        (image_hbm, image_ref),
        (turn_hbm, turn_ref),
        (twist_hbm, twist_ref),
        (interval_hbm, interval_ref),
        (station_p_hbm, station_p_ref),
        (station_q_hbm, station_q_ref),
        (live_hbm, live_ref),
        (weight_hbm, weight_ref),
        (vis_hbm, vis_ref),
    )
    loads = [
        pltpu.make_async_copy(source, target, load_sem.at[place])
        for place, (source, target) in enumerate(order)
    ]
    for load in loads:
        load.start()

    ring_z, ring_y = n_vis // 4, n_facet // 2
    side = me // (2 * ring_z)
    vis_steps = [
        (away, along, core)
        for away in range(2)
        for along in range(ring_z)
        for core in range(2)
        if (away, along, core) != (0, 0, 0)
    ]
    vis_steps.sort(key=lambda step: (-2 * step[0] - min(step[1], ring_z - step[1]), -step[2]))
    facet_steps = [(along, away) for along in range(ring_y) for away in range(2) if along or away]
    facet_steps.sort(key=lambda step: -min(step[0], ring_y - step[0]) - step[1])

    def vis_peer(step):
        away, along, core = step
        z = lax.rem(me // 2 + along, ring_z)
        return ((side ^ away) * ring_z + z) * 2 + ((me & 1) ^ core)

    def facet_peer(step):
        along, away = step
        return lax.rem(facet // 2 + along, ring_y) * 2 + ((facet & 1) ^ away)

    barrier = pltpu.get_barrier_semaphore()
    for step in vis_steps:
        pl.semaphore_signal(barrier, 1, device_id=(vis_peer(step), facet), device_id_type=MESH)
    for step in facet_steps:
        pl.semaphore_signal(barrier, 1, device_id=(me, facet_peer(step)), device_id_type=MESH)

    def send_all(source, target, send_sem, recv_sem):
        for step in vis_steps:
            peer = vis_peer(step)
            pltpu.make_async_remote_copy(
                src_ref=source(peer),
                dst_ref=target.at[me],
                send_sem=send_sem,
                recv_sem=recv_sem(step),
                device_id=(peer, facet),
                device_id_type=MESH,
            ).start()

    def wait_blocks(buffer, count, sem):
        view = buffer.at[pl.ds(0, count)]
        pltpu.make_async_copy(view, view, sem).wait()

    def pair_row(pair):
        return lax.rem(pair, 4) * 4 + pair // 4

    loads[0].wait()
    loads[1].wait()

    def group_place(group):
        return group // 4, pl.ds(pl.multiple_of(lax.rem(group, 4) * 128, 128), 128)

    def order_cells(group, carry):
        place, lanes = group_place(group)

        def read(holder):
            rows = pl.ds(holder * 4, 4)
            return jnp.concatenate([cell_row_ref[rows, :], cell_col_ref[rows, :]], axis=0)

        for turn, rows in enumerate(slots_to_pairs([read(4 * group + k) for k in range(4)])):
            lane = lax.broadcasted_iota(jnp.int32, (4, 128), 1)
            local_row[place, 4 * turn : 4 * turn + 4, lanes] = rows[0:4] + ((lane >> 4) & 1) * 64
            local_col[place, 4 * turn : 4 * turn + 4, lanes] = rows[4:8]
        return carry

    lax.fori_loop(0, n_vis // 4, order_cells, 0, unroll=4)
    for place in range(2):
        cos, sin = unit_phase((local_col[place] * 8) & (SIDE - 1))
        step_cos[place] = cos
        step_sin[place] = sin

    loads[2].wait()
    intervals_here = gain_ref.shape[1]
    stations = gain_ref.shape[2]
    gain_all[me] = jnp.zeros((8, 256), F32)
    for comp in range(8):
        half, lane = comp // 4, 64 * (comp % 4)
        gain_all[me, 4 * half : 4 * half + intervals_here, lane : lane + stations] = gain_ref[comp]

    pl.semaphore_wait(barrier, n_vis + n_facet - 2)
    send_all(lambda peer: gain_all.at[me], gain_all, gain_send, lambda step: gain_recv)

    loads[3].wait()
    lines[...] = image_ref[...].T
    loads[4].wait()
    loads[5].wait()
    first_hi = jnp.concatenate([turn_ref[:INNER], turn_ref[INNER : 2 * INNER]], axis=1)
    first_lo = jnp.concatenate([turn_ref[2 * INNER : 3 * INNER], turn_ref[3 * INNER :]], axis=1)
    first_twice = jnp.concatenate([first_hi, first_hi], axis=0)
    group_b = 8
    for start in range(0, RADIX, group_b):
        halves = [
            split_pair(lines[pl.ds(b, INNER, stride=RADIX), :].T)
            for b in range(start, start + group_b)
        ]
        high = jnp.concatenate([pair[0] for pair in halves], axis=0)
        low = jnp.concatenate([pair[1] for pair in halves], axis=0)
        both = matmul(jnp.concatenate([high, low], axis=1), first_twice) + matmul(high, first_lo)
        for place in range(group_b):
            b = start + place
            here = both[place * side_x : (place + 1) * side_x]
            re, im = here[:, :INNER], here[:, INNER:]
            cos = twist_ref[0, b : b + 1, :]
            sin = twist_ref[1, b : b + 1, :]
            work_re[b] = re * cos + im * sin
            work_im[b] = im * cos - re * sin

    def forward_rows(chunk, carry):
        rows = pl.ds(pl.multiple_of(chunk * 8, 8), 8)
        rows_im = pl.ds(pl.multiple_of(side_x + chunk * 8, 8), 8)
        vals = radix16([(work_re[b, rows, :], work_im[b, rows, :]) for b in range(RADIX)], -1.0)
        for q in range(RADIX):
            table[q, rows, :] = vals[q][0]
            table[q, rows_im, :] = vals[q][1]
        return carry

    lax.fori_loop(0, side_x // 8, forward_rows, 0, unroll=4)

    chunk_w = 256
    by_lanes = 256
    blocks_x = side_x // 8

    def hot_columns(local):
        index = lax.broadcasted_iota(jnp.int32, (INNER, local.shape[1]), 0)
        return jnp.where(index == local, 1.0, 0.0).astype(BF16)

    def value_row(pair):
        return lax.rem(pair, 4) * 4 + lax.rem(pair // 4, 2)

    def forward_pair(pair, carry):
        half = pair // 8
        row = pl.ds(pair_row(pair), 1)
        high, low = split_pair(table[pair])
        both = jnp.concatenate([high, low], axis=0)

        def picked_by_matmul(local):
            picked = matmul(both, hot_columns(local))
            picked = picked[: 2 * side_x] + picked[2 * side_x :]
            return lambda first: picked[first : first + 8]

        def picked_by_lanes(local):
            index = jnp.broadcast_to(local, (8, INNER))
            return lambda first: pick_lanes(table[pair, first : first + 8, :], index)

        pieces = [(start, INNER, picked_by_lanes) for start in range(0, by_lanes, INNER)]
        pieces += [(start, 256, picked_by_matmul) for start in range(by_lanes, width, 256)]
        for place in range(2):
            out_re = []
            out_im = []
            whole_index = local_row[place, row, :]
            whole_column = local_col[place, row, :]
            whole_cos = step_cos[place, row, :]
            whole_sin = step_sin[place, row, :]
            x_index = me * side_x + lax.broadcasted_iota(jnp.int32, (8, width), 0)
            all_cos, all_sin = unit_phase((whole_column * x_index) & (SIDE - 1))
            fine_cos[pair, place] = all_cos
            fine_sin[pair, place] = all_sin
            for start, size, picker in pieces:
                lanes = slice(start, start + size)
                pick = picker(whole_index[:, lanes])
                cos = jnp.broadcast_to(whole_cos[:, lanes], (8, size))
                sin = jnp.broadcast_to(whole_sin[:, lanes], (8, size))
                sum_re = pick(8 * blocks_x - 8)
                sum_im = pick(side_x + 8 * blocks_x - 8)
                for block in range(blocks_x - 2, -1, -1):
                    re = pick(8 * block)
                    im = pick(side_x + 8 * block)
                    sum_re, sum_im = (
                        re + (sum_re * cos + sum_im * sin),
                        im + (sum_im * cos - sum_re * sin),
                    )
                cos = all_cos[:, lanes]
                sin = all_sin[:, lanes]
                out_re.append(jnp.sum(sum_re * cos + sum_im * sin, axis=0, keepdims=True))
                out_im.append(jnp.sum(sum_im * cos - sum_re * sin, axis=0, keepdims=True))
            re_row = pl.ds(value_row(pair), 1)
            im_row = pl.ds(value_row(pair) + 2, 1)
            values[half, place, re_row, :] = jnp.concatenate(out_re, axis=1)
            values[half, place, im_row, :] = jnp.concatenate(out_im, axis=1)
        return carry

    for half in range(2):
        lax.fori_loop(8 * half, 8 * half + 8, forward_pair, 0, unroll=4)

        def pack_values(group, carry):
            place, lanes = group_place(group)
            rows = [values[half, place, 4 * turn : 4 * turn + 4, lanes] for turn in range(4)]
            for member, block in enumerate(pairs_to_slots(rows)):
                part_out[half, 4 * group + member] = block
            return carry

        lax.fori_loop(0, n_vis // 4, pack_values, 0, unroll=8)
        send_all(
            lambda peer: part_out.at[half, peer],
            part_in.at[half],
            part_send.at[half],
            lambda step: part_recv.at[half],
        )
        part_in[half, me] = part_out[half, me]

    for load in loads[6:]:
        load.wait()
    wait_blocks(gain_all, n_vis - 1, gain_recv)
    high, low = split_pair(gain_all[...].reshape(n_vis * 8, 256).T)
    both = jnp.concatenate([high, low], axis=0)
    interval = wide_row(interval_ref[...])
    gain_row = (interval >> 2) * 8 + (interval & 3)
    station = lax.broadcasted_iota(jnp.int32, (64, slots), 0)
    at_p = jnp.where(station == wide_row(station_p_ref[...]), 1.0, 0.0)
    at_q = jnp.where(station == wide_row(station_q_ref[...]), 1.0, 0.0)
    index = lax.broadcasted_iota(jnp.int32, (n_vis * 8, slots), 0)
    jones_p = []
    jones_q = []
    for half in range(2):
        hot = jnp.where(index == gain_row + 4 * half, 1.0, 0.0).astype(BF16)
        picked = matmul(both, hot)
        picked = picked[:256] + picked[256:]
        for comp in range(4):
            here = picked[64 * comp : 64 * comp + 64]
            jones_p.append(jnp.sum(here * at_p, axis=0, keepdims=True))
            jones_q.append(jnp.sum(here * at_q, axis=0, keepdims=True))
    outer_re, outer_im = jones_outer(jones_p, jones_q)
    live = wide_row(live_ref[...]).astype(F32)
    scale = wide_row(weight_ref[...]) * live

    for half in range(2):
        here = slice(half * part, (half + 1) * part)
        wait_blocks(part_in.at[half], n_vis - 1, part_recv.at[half])
        model = jnp.sum(part_in[half], axis=0) * (1.0 / SIDE)
        model_re = wide_row(model[0:2])
        model_im = wide_row(model[2:4])
        own_re, own_im = outer_re[:, here], outer_im[:, here]
        pred_in[half, facet, 0:4, :] = model_re * own_re - model_im * own_im
        pred_in[half, facet, 4:8, :] = model_re * own_im + model_im * own_re

        for step in facet_steps:
            pltpu.make_async_remote_copy(
                src_ref=pred_in.at[half, facet],
                dst_ref=pred_in.at[half, facet],
                send_sem=pred_send.at[half],
                recv_sem=pred_recv.at[half],
                device_id=(me, facet_peer(step)),
                device_id_type=MESH,
            ).start()

    for half in range(2):
        here = slice(half * part, (half + 1) * part)
        wait_blocks(pred_in.at[half], n_facet - 1, pred_recv.at[half])
        predicted = pred_in[half, 0]
        for other in range(1, n_facet):
            predicted = predicted + pred_in[half, other]
        resid = (vis_ref[:, here] - predicted) * live[:, here]
        resid_ref[:, here] = resid
        stokes_re, stokes_im = jones_stokes(
            [gain[:, here] for gain in jones_p],
            [gain[:, here] for gain in jones_q],
            [resid[comp : comp + 1] for comp in range(8)],
        )
        stokes_in[half, me, 0:2, :] = tall_block(stokes_re * scale[:, here])
        stokes_in[half, me, 2:4, :] = tall_block(stokes_im * scale[:, here])
        send_all(
            lambda peer: stokes_in.at[half, me],
            stokes_in.at[half],
            stokes_send.at[half],
            lambda step: stokes_recv.at[half, step[0]],
        )

    def backward_pair(pair, place, first):
        total = jnp.zeros((4 * side_x, INNER), F32)
        half = pair // 8
        row = pl.ds(pair_row(pair), 1)
        whole_re = values[half, place, pl.ds(value_row(pair), 1), :]
        whole_im = values[half, place, pl.ds(value_row(pair) + 2, 1), :]
        whole_index = local_row[place, row, :]
        whole_cos = step_cos[place, row, :]
        whole_sin = step_sin[place, row, :]
        for start in range(0, width, chunk_w):
            lanes = slice(start, start + chunk_w)
            re = whole_re[:, lanes]
            im = whole_im[:, lanes]
            cos = fine_cos[pair, place, :, lanes]
            sin = fine_sin[pair, place, :, lanes]
            real_rows = [re * cos - im * sin]
            imag_rows = [re * sin + im * cos]
            cos = jnp.broadcast_to(whole_cos[:, lanes], (8, chunk_w))
            sin = jnp.broadcast_to(whole_sin[:, lanes], (8, chunk_w))
            for _ in range(blocks_x - 1):
                re, im = real_rows[-1], imag_rows[-1]
                real_rows.append(re * cos - im * sin)
                imag_rows.append(re * sin + im * cos)
            high, low = split_pair(jnp.concatenate(real_rows + imag_rows, axis=0))
            both = jnp.concatenate([high, low], axis=0)
            total = total + lax.dot_general(
                both,
                hot_columns(whole_index[:, lanes]),
                (((1,), (1,)), ((), ())),
                preferred_element_type=F32,
            )
        total = total[: 2 * side_x] + total[2 * side_x :]
        table[pair] = total if first else table[pair] + total

    for half in range(2):
        for away in range(2):
            place = side ^ away
            count = n_vis // 2 - (1 - away)
            wait_blocks(stokes_in.at[half], count, stokes_recv.at[half, away])

            def order_stokes(group, carry):
                lanes = pl.ds(pl.multiple_of(group * 128, 128), 128)
                first = place * (n_vis // 2) + 4 * group
                blocks = [stokes_in[half, first + member] for member in range(4)]
                for turn, rows in enumerate(slots_to_pairs(blocks)):
                    values[half, place, 4 * turn : 4 * turn + 4, lanes] = rows
                return carry

            def backward(pair, carry):
                backward_pair(pair, place, away == 0)
                return carry

            lax.fori_loop(0, n_vis // 8, order_stokes, 0, unroll=4)
            lax.fori_loop(8 * half, 8 * half + 8, backward, 0, unroll=8)

    wait_blocks(gain_all, n_vis - 1, gain_send)
    for half in range(2):
        wait_blocks(part_in.at[half], n_vis - 1, part_send.at[half])
        wait_blocks(pred_in.at[half], n_facet - 1, pred_send.at[half])
        wait_blocks(stokes_in.at[half], n_vis - 1, stokes_send.at[half])


def image_kernel(
    factor,
    resid_ref,
    table,
    turn_ref,
    twist_ref,
    resid_hbm,
    dirty_hbm,
    work_re,
    work_im,
    lines,
    dirty,
    resid_sem,
    dirty_sem,
):
    side_x = dirty.shape[0]
    keep = pltpu.make_async_copy(resid_ref, resid_hbm, resid_sem)
    keep.start()

    def backward_rows(chunk, carry):
        rows = pl.ds(pl.multiple_of(chunk * 8, 8), 8)
        rows_im = pl.ds(pl.multiple_of(side_x + chunk * 8, 8), 8)
        vals = radix16([(table[q, rows, :], table[q, rows_im, :]) for q in range(RADIX)], 1.0)
        for b in range(RADIX):
            re, im = vals[b]
            cos = twist_ref[0, b : b + 1, :]
            sin = twist_ref[1, b : b + 1, :]
            work_re[b, rows, :] = re * cos - im * sin
            work_im[b, rows, :] = re * sin + im * cos
        return carry

    lax.fori_loop(0, side_x // 8, backward_rows, 0, unroll=8)

    last_hi = turn_ref[: 2 * INNER]
    last_lo = turn_ref[2 * INNER :]
    last_both = jnp.concatenate([last_hi, last_lo], axis=1)
    group_b = 8
    for start in range(0, RADIX, group_b):
        halves = [
            split_pair(jnp.concatenate([work_re[b], work_im[b]], axis=1))
            for b in range(start, start + group_b)
        ]
        high = jnp.concatenate([pair[0] for pair in halves], axis=0)
        low = jnp.concatenate([pair[1] for pair in halves], axis=0)
        both = matmul(high, last_both)
        part = (both[:, :INNER] + (both[:, INNER:] + matmul(low, last_hi))) * factor
        for place in range(group_b):
            here = part[place * side_x : (place + 1) * side_x]
            lines[pl.ds(start + place, INNER, stride=RADIX), :] = here.T
    count = dirty_sem.shape[0]
    wide = SIDE // count
    copies = []
    for piece in range(count):
        here = slice(piece * wide, (piece + 1) * wide)
        dirty[:, here] = lines[here, :].T
        copies.append(
            pltpu.make_async_copy(dirty.at[:, here], dirty_hbm.at[:, here], dirty_sem.at[piece])
        )
        copies[-1].start()
    for copy in copies:
        copy.wait()
    keep.wait()


def per_device(
    visibilities,
    weights,
    live_slots,
    station_p,
    station_q,
    interval,
    cell_row,
    cell_col,
    jones_gains,
    model_image,
):
    n_vis = lax.axis_size("vis")
    n_facet = lax.axis_size("facet")
    side_x = model_image.shape[1]
    slots = visibilities.shape[1]
    width = n_vis * slots // RADIX // 2

    def rows_of(array):
        return array.reshape(-1, 128)

    turn, twist = [jnp.asarray(table) for table in make_tables()]
    given = [
        visibilities,
        rows_of(weights),
        rows_of(live_slots),
        rows_of(station_p),
        rows_of(station_q),
        rows_of(interval),
        rows_of(cell_row),
        rows_of(cell_col),
        jones_gains[0],
        model_image[0],
        turn,
        twist,
    ]
    in_hbm = pl.BlockSpec(memory_space=pltpu.HBM)
    in_vmem = pl.BlockSpec(memory_space=pltpu.VMEM)
    work = pltpu.VMEM((RADIX, side_x, INNER), F32)
    kept = pl.pallas_call(
        functools.partial(exchange_kernel, n_vis, n_facet),
        out_shape=(
            pltpu.VMEM((8, slots), F32),
            pltpu.VMEM((RADIX, 2 * side_x, INNER), F32),
            pltpu.VMEM(turn.shape, turn.dtype),
            pltpu.VMEM(twist.shape, twist.dtype),
        ),
        in_specs=[in_hbm] * len(given),
        out_specs=(in_vmem,) * 4,
        scratch_shapes=[pltpu.VMEM(array.shape, array.dtype) for array in given[:-2]]
        + [
            pltpu.VMEM((n_vis, 8, 256), F32),
            pltpu.VMEM((2, n_vis, 4, 128), F32),
            pltpu.VMEM((2, n_vis, 4, 128), F32),
            pltpu.VMEM((2, n_facet, 8, slots // 2), F32),
            pltpu.VMEM((2, n_vis, 4, 128), F32),
            pltpu.VMEM((SIDE, side_x), F32),
            work,
            work,
            pltpu.VMEM((2, 16, width), jnp.int32),
            pltpu.VMEM((2, 16, width), jnp.int32),
            pltpu.VMEM((2, 2, 16, width), F32),
            pltpu.VMEM((2, 16, width), F32),
            pltpu.VMEM((2, 16, width), F32),
            pltpu.VMEM((RADIX, 2, 8, width), F32),
            pltpu.VMEM((RADIX, 2, 8, width), F32),
            pltpu.SemaphoreType.DMA((len(given),)),
            pltpu.SemaphoreType.DMA(()),
            pltpu.SemaphoreType.DMA(()),
        ]
        + [pltpu.SemaphoreType.DMA((2,))] * 5
        + [pltpu.SemaphoreType.DMA((2, 2))],
        compiler_params=pltpu.CompilerParams(
            collective_id=0, has_side_effects=True, vmem_limit_bytes=40 * 1024 * 1024
        ),
    )(*[pltpu.with_memory_space_constraint(array, pltpu.HBM) for array in given])
    resid, dirty = pl.pallas_call(
        functools.partial(image_kernel, 4.0 / math.sqrt(slots * n_vis)),
        out_shape=(
            pltpu.HBM((8, slots), F32),
            pltpu.HBM((side_x, SIDE), F32),
        ),
        in_specs=[in_vmem] * 4,
        out_specs=(in_hbm, in_hbm),
        scratch_shapes=[
            work,
            work,
            pltpu.VMEM((SIDE, side_x), F32),
            pltpu.VMEM((side_x, SIDE), F32),
            pltpu.SemaphoreType.DMA(()),
            pltpu.SemaphoreType.DMA((4,)),
        ],
        compiler_params=pltpu.CompilerParams(vmem_limit_bytes=40 * 1024 * 1024),
    )(*kept)
    return resid, dirty[None]


def solution(mesh):
    return jax.shard_map(
        per_device,
        mesh=mesh,
        in_specs=(
            P(None, "vis"),
            P("vis"),
            P("vis"),
            P("vis"),
            P("vis"),
            P("vis"),
            P(),
            P(),
            P("facet", None, "vis", None),
            P("facet", "vis", None),
        ),
        out_specs=(P(None, "vis"), P("facet", "vis", None)),
        check_vma=False,
    )
```

```python
import functools
import math

import jax
import jax.numpy as jnp
import numpy as np
from jax import lax
from jax.experimental import pallas as pl
from jax.experimental.pallas import tpu as pltpu
from jax.sharding import PartitionSpec as P

TWO_PI = 2.0 * math.pi
MESH = pl.DeviceIdType.MESH
F32 = jnp.float32
BF16 = jnp.bfloat16

RADIX = 16
INNER = 128
SIDE = RADIX * INNER


def split_table(table):
    high = table.astype(BF16)
    low = (table - high.astype(np.float64)).astype(BF16)
    return high, low


def make_tables():
    inner = np.arange(INNER)
    angle = TWO_PI * (np.outer(inner, inner) % INNER) / INNER
    turn = np.concatenate([np.cos(angle), -np.sin(angle)], axis=0)
    twist = TWO_PI * np.outer(np.arange(RADIX), inner) / SIDE
    twist = np.stack([np.cos(twist), np.sin(twist)]).astype(np.float32)
    return np.concatenate(split_table(turn), axis=0), twist


def split_pair(value):
    high = value.astype(BF16)
    low = (value - high.astype(F32)).astype(BF16)
    return high, low


def matmul(left, right):
    return jnp.dot(left, right, preferred_element_type=F32)


def cmul_const(pair, real, imag):
    re, im = pair
    return re * real - im * imag, re * imag + im * real


def radix4(vals, sign):
    (ar, ai), (br, bi), (cr, ci), (dr, di) = vals
    sr, si = ar + cr, ai + ci
    tr, ti = ar - cr, ai - ci
    ur, ui = br + dr, bi + di
    wr, wi = br - dr, bi - di
    if sign < 0:
        xr, xi = wi, -wr
    else:
        xr, xi = -wi, wr
    return [(sr + ur, si + ui), (tr + xr, ti + xi), (sr - ur, si - ui), (tr - xr, ti - xi)]


def radix16(vals, sign):
    inner = [radix4([vals[4 * n1 + n2] for n1 in range(4)], sign) for n2 in range(4)]
    out = [None] * 16
    for k1 in range(4):
        column = []
        for n2 in range(4):
            turn = n2 * k1
            value = inner[n2][k1]
            if turn == 4:
                re, im = value
                value = (im, -re) if sign < 0 else (-im, re)
            elif turn == 2 or turn == 6:
                half = math.sqrt(0.5)
                re, im = value
                if sign < 0:
                    value = ((re + im) * half, (im - re) * half)
                else:
                    value = ((re - im) * half, (re + im) * half)
                if turn == 6:
                    re, im = value
                    value = (im, -re) if sign < 0 else (-im, re)
            elif turn:
                angle = sign * TWO_PI * turn / 16
                value = cmul_const(value, math.cos(angle), math.sin(angle))
            column.append(value)
        for k2, value in enumerate(radix4(column, sign)):
            out[k1 + 4 * k2] = value
    return out


def unit_phase(step):
    quarter = (step + 256) >> 9
    angle = (step - (quarter << 9)).astype(F32) * (TWO_PI / SIDE)
    square = angle * angle
    sine = angle * (
        1.0
        + square
        * (-1.6666654611e-1 + square * (8.3321608736e-3 + square * -1.9515295891e-4))
    )
    cosine = 1.0 + square * (
        -0.5
        + square
        * (4.166664568298827e-2 + square * (-1.388731625493765e-3 + square * 2.443315711809948e-5))
    )
    odd = (quarter & 1) == 1
    cos_mag = jnp.where(odd, sine, cosine)
    sin_mag = jnp.where(odd, cosine, sine)
    cos_val = jnp.where(((quarter + 1) & 2) == 2, -cos_mag, cos_mag)
    sin_val = jnp.where((quarter & 2) == 2, -sin_mag, sin_mag)
    return cos_val, sin_val


def pick_lanes(value, index):
    numbers = lax.GatherDimensionNumbers(
        offset_dims=(),
        collapsed_slice_dims=(1,),
        start_index_map=(1,),
        operand_batching_dims=(0,),
        start_indices_batching_dims=(0,),
    )
    return lax.gather(
        value,
        index[..., None],
        numbers,
        slice_sizes=(1, 1),
        mode=lax.GatherScatterMode.PROMISE_IN_BOUNDS,
    )


def lane_block(shape):
    return lax.broadcasted_iota(jnp.int32, shape, 1) >> 5


def slots_to_pairs(blocks):
    where = lane_block(blocks[0].shape)
    rows = []
    for turn in range(4):
        total = None
        for member in range(4):
            shift = 32 * (member - turn) % 128
            moved = pltpu.roll(blocks[member], shift, 1) if shift else blocks[member]
            total = moved if total is None else jnp.where(where == member, moved, total)
        rows.append(total)
    return rows


def pairs_to_slots(rows):
    where = lane_block(rows[0].shape)
    blocks = []
    for member in range(4):
        total = None
        for turn in range(4):
            shift = 32 * (turn - member) % 128
            moved = pltpu.roll(rows[turn], shift, 1) if shift else rows[turn]
            total = moved if total is None else jnp.where(where == turn, moved, total)
        blocks.append(total)
    return blocks


def wide_row(block):
    return jnp.concatenate([block[k : k + 1, :] for k in range(block.shape[0])], axis=1)


def tall_block(row):
    count = row.shape[1] // 128
    return jnp.concatenate([row[:, 128 * k : 128 * (k + 1)] for k in range(count)], axis=0)


def jones_outer(left, right):
    real_rows = []
    imag_rows = []
    for row_a in range(2):
        for row_b in range(2):
            real_sum = 0.0
            imag_sum = 0.0
            for inner in range(2):
                left_re = left[row_a * 2 + inner]
                left_im = left[4 + row_a * 2 + inner]
                right_re = right[row_b * 2 + inner]
                right_im = right[4 + row_b * 2 + inner]
                real_sum = real_sum + left_re * right_re + left_im * right_im
                imag_sum = imag_sum + left_im * right_re - left_re * right_im
            real_rows.append(real_sum)
            imag_rows.append(imag_sum)
    return jnp.concatenate(real_rows, axis=0), jnp.concatenate(imag_rows, axis=0)


def jones_stokes(left, right, resid):
    total_re = 0.0
    total_im = 0.0
    for inner in range(2):
        for row_a in range(2):
            for row_b in range(2):
                left_re = left[row_a * 2 + inner]
                left_im = left[4 + row_a * 2 + inner]
                res_re = resid[row_a * 2 + row_b]
                res_im = resid[4 + row_a * 2 + row_b]
                right_re = right[row_b * 2 + inner]
                right_im = right[4 + row_b * 2 + inner]
                mid_re = left_re * res_re + left_im * res_im
                mid_im = left_re * res_im - left_im * res_re
                total_re = total_re + mid_re * right_re - mid_im * right_im
                total_im = total_im + mid_re * right_im + mid_im * right_re
    return 0.5 * total_re, 0.5 * total_im


def exchange_kernel(
    n_vis,
    n_facet,
    vis_hbm,
    weight_hbm,
    live_hbm,
    station_p_hbm,
    station_q_hbm,
    interval_hbm,
    cell_row_hbm,
    cell_col_hbm,
    gain_hbm,
    image_hbm,
    turn_hbm,
    twist_hbm,
    resid_ref,
    table,
    turn_ref,
    twist_ref,
    vis_ref,
    weight_ref,
    live_ref,
    station_p_ref,
    station_q_ref,
    interval_ref,
    cell_row_ref,
    cell_col_ref,
    gain_ref,
    image_ref,
    gain_all,
    part_out,
    part_in,
    pred_in,
    stokes_in,
    lines,
    work_re,
    work_im,
    local_row,
    local_col,
    values,
    step_cos,
    step_sin,
    fine_cos,
    fine_sin,
    load_sem,
    gain_send,
    gain_recv,
    part_send,
    part_recv,
    pred_send,
    pred_recv,
    stokes_send,
    stokes_recv,
):
    me = lax.axis_index("vis")
    facet = lax.axis_index("facet")
    side_x = image_ref.shape[0]
    width = values.shape[3]
    slots = vis_ref.shape[1]
    part = slots // 2

    order = (
        (cell_row_hbm, cell_row_ref),
        (cell_col_hbm, cell_col_ref),
        (gain_hbm, gain_ref),
        (image_hbm, image_ref),
        (turn_hbm, turn_ref),
        (twist_hbm, twist_ref),
        (interval_hbm, interval_ref),
        (station_p_hbm, station_p_ref),
        (station_q_hbm, station_q_ref),
        (live_hbm, live_ref),
        (weight_hbm, weight_ref),
        (vis_hbm, vis_ref),
    )
    loads = [
        pltpu.make_async_copy(source, target, load_sem.at[place])
        for place, (source, target) in enumerate(order)
    ]
    for load in loads:
        load.start()

    ring_z, ring_y = n_vis // 4, n_facet // 2
    side = me // (2 * ring_z)
    vis_steps = [
        (away, along, core)
        for away in range(2)
        for along in range(ring_z)
        for core in range(2)
        if (away, along, core) != (0, 0, 0)
    ]
    vis_steps.sort(key=lambda step: (-2 * step[0] - min(step[1], ring_z - step[1]), -step[2]))
    facet_steps = [(along, away) for along in range(ring_y) for away in range(2) if along or away]
    facet_steps.sort(key=lambda step: -min(step[0], ring_y - step[0]) - step[1])

    def vis_peer(step):
        away, along, core = step
        z = lax.rem(me // 2 + along, ring_z)
        return ((side ^ away) * ring_z + z) * 2 + ((me & 1) ^ core)

    def facet_peer(step):
        along, away = step
        return lax.rem(facet // 2 + along, ring_y) * 2 + ((facet & 1) ^ away)

    barrier = pltpu.get_barrier_semaphore()
    for step in vis_steps:
        pl.semaphore_signal(barrier, 1, device_id=(vis_peer(step), facet), device_id_type=MESH)
    for step in facet_steps:
        pl.semaphore_signal(barrier, 1, device_id=(me, facet_peer(step)), device_id_type=MESH)

    def send_all(source, target, send_sem, recv_sem):
        for step in vis_steps:
            peer = vis_peer(step)
            pltpu.make_async_remote_copy(
                src_ref=source(peer),
                dst_ref=target.at[me],
                send_sem=send_sem,
                recv_sem=recv_sem(step),
                device_id=(peer, facet),
                device_id_type=MESH,
            ).start()

    def wait_blocks(buffer, count, sem):
        view = buffer.at[pl.ds(0, count)]
        pltpu.make_async_copy(view, view, sem).wait()

    def pair_row(pair):
        return lax.rem(pair, 4) * 4 + pair // 4

    loads[0].wait()
    loads[1].wait()

    def group_place(group):
        return group // 4, pl.ds(pl.multiple_of(lax.rem(group, 4) * 128, 128), 128)

    def order_cells(group, carry):
        place, lanes = group_place(group)

        def read(holder):
            rows = pl.ds(holder * 4, 4)
            return jnp.concatenate([cell_row_ref[rows, :], cell_col_ref[rows, :]], axis=0)

        for turn, rows in enumerate(slots_to_pairs([read(4 * group + k) for k in range(4)])):
            lane = lax.broadcasted_iota(jnp.int32, (4, 128), 1)
            local_row[place, 4 * turn : 4 * turn + 4, lanes] = rows[0:4] + ((lane >> 4) & 1) * 64
            local_col[place, 4 * turn : 4 * turn + 4, lanes] = rows[4:8]
        return carry

    lax.fori_loop(0, n_vis // 4, order_cells, 0, unroll=4)
    for place in range(2):
        cos, sin = unit_phase((local_col[place] * 8) & (SIDE - 1))
        step_cos[place] = cos
        step_sin[place] = sin

    def fine_phases(pair, carry):
        x_index = me * side_x + lax.broadcasted_iota(jnp.int32, (8, width), 0)
        for place in range(2):
            column = local_col[place, pl.ds(pair_row(pair), 1), :]
            cos, sin = unit_phase((column * x_index) & (SIDE - 1))
            fine_cos[pair, place] = cos
            fine_sin[pair, place] = sin
        return carry

    lax.fori_loop(0, RADIX, fine_phases, 0, unroll=4)

    loads[2].wait()
    intervals_here = gain_ref.shape[1]
    stations = gain_ref.shape[2]
    core, chip = me & 1, me // 2
    gain_all[core, chip] = jnp.zeros((8, 256), F32)
    for comp in range(8):
        half, lane = comp // 4, 64 * (comp % 4)
        rows = slice(4 * half, 4 * half + intervals_here)
        gain_all[core, chip, rows, lane : lane + stations] = gain_ref[comp]

    loads[3].wait()
    lines[...] = image_ref[...].T
    loads[4].wait()
    loads[5].wait()
    first_hi = jnp.concatenate([turn_ref[:INNER], turn_ref[INNER : 2 * INNER]], axis=1)
    first_lo = jnp.concatenate([turn_ref[2 * INNER : 3 * INNER], turn_ref[3 * INNER :]], axis=1)
    first_twice = jnp.concatenate([first_hi, first_hi], axis=0)
    group_b = 8
    for start in range(0, RADIX, group_b):
        halves = [
            split_pair(lines[pl.ds(b, INNER, stride=RADIX), :].T)
            for b in range(start, start + group_b)
        ]
        high = jnp.concatenate([pair[0] for pair in halves], axis=0)
        low = jnp.concatenate([pair[1] for pair in halves], axis=0)
        both = matmul(jnp.concatenate([high, low], axis=1), first_twice) + matmul(high, first_lo)
        for place in range(group_b):
            b = start + place
            here = both[place * side_x : (place + 1) * side_x]
            re, im = here[:, :INNER], here[:, INNER:]
            cos = twist_ref[0, b : b + 1, :]
            sin = twist_ref[1, b : b + 1, :]
            work_re[b] = re * cos + im * sin
            work_im[b] = im * cos - re * sin

    def forward_rows(chunk, carry):
        rows = pl.ds(pl.multiple_of(chunk * 8, 8), 8)
        rows_im = pl.ds(pl.multiple_of(side_x + chunk * 8, 8), 8)
        vals = radix16([(work_re[b, rows, :], work_im[b, rows, :]) for b in range(RADIX)], -1.0)
        for q in range(RADIX):
            table[q, rows, :] = vals[q][0]
            table[q, rows_im, :] = vals[q][1]
        return carry

    lax.fori_loop(0, side_x // 8, forward_rows, 0, unroll=4)

    pl.semaphore_wait(barrier, n_vis + n_facet - 2)
    for step in vis_steps:
        if step[2] == 0:
            pltpu.make_async_remote_copy(
                src_ref=gain_all.at[core, chip],
                dst_ref=gain_all.at[core, chip],
                send_sem=gain_send.at[0],
                recv_sem=gain_recv.at[0],
                device_id=(vis_peer(step), facet),
                device_id_type=MESH,
            ).start()

    chunk_w = 256
    by_lanes = 256
    blocks_x = side_x // 8

    def hot_columns(local):
        index = lax.broadcasted_iota(jnp.int32, (INNER, local.shape[1]), 0)
        return jnp.where(index == local, 1.0, 0.0).astype(BF16)

    def value_row(pair):
        return lax.rem(pair, 4) * 4 + lax.rem(pair // 4, 2)

    def forward_pair(pair, carry):
        half = pair // 8
        row = pl.ds(pair_row(pair), 1)
        high, low = split_pair(table[pair])
        both = jnp.concatenate([high, low], axis=0)

        def picked_by_matmul(local):
            picked = matmul(both, hot_columns(local))
            picked = picked[: 2 * side_x] + picked[2 * side_x :]
            return lambda first: picked[first : first + 8]

        def picked_by_lanes(local):
            index = jnp.broadcast_to(local, (8, INNER))
            return lambda first: pick_lanes(table[pair, first : first + 8, :], index)

        pieces = [(start, INNER, picked_by_lanes) for start in range(0, by_lanes, INNER)]
        pieces += [(start, 256, picked_by_matmul) for start in range(by_lanes, width, 256)]
        for place in range(2):
            out_re = []
            out_im = []
            whole_index = local_row[place, row, :]
            whole_cos = step_cos[place, row, :]
            whole_sin = step_sin[place, row, :]
            all_cos = fine_cos[pair, place]
            all_sin = fine_sin[pair, place]
            for start, size, picker in pieces:
                lanes = slice(start, start + size)
                pick = picker(whole_index[:, lanes])
                cos = jnp.broadcast_to(whole_cos[:, lanes], (8, size))
                sin = jnp.broadcast_to(whole_sin[:, lanes], (8, size))
                sum_re = pick(8 * blocks_x - 8)
                sum_im = pick(side_x + 8 * blocks_x - 8)
                for block in range(blocks_x - 2, -1, -1):
                    re = pick(8 * block)
                    im = pick(side_x + 8 * block)
                    sum_re, sum_im = (
                        re + (sum_re * cos + sum_im * sin),
                        im + (sum_im * cos - sum_re * sin),
                    )
                cos = all_cos[:, lanes]
                sin = all_sin[:, lanes]
                out_re.append(jnp.sum(sum_re * cos + sum_im * sin, axis=0, keepdims=True))
                out_im.append(jnp.sum(sum_im * cos - sum_re * sin, axis=0, keepdims=True))
            re_row = pl.ds(value_row(pair), 1)
            im_row = pl.ds(value_row(pair) + 2, 1)
            values[half, place, re_row, :] = jnp.concatenate(out_re, axis=1)
            values[half, place, im_row, :] = jnp.concatenate(out_im, axis=1)
        return carry

    for half in range(2):
        lax.fori_loop(8 * half, 8 * half + 8, forward_pair, 0, unroll=8)

        def pack_values(group, carry):
            place, lanes = group_place(group)
            rows = [values[half, place, 4 * turn : 4 * turn + 4, lanes] for turn in range(4)]
            for member, block in enumerate(pairs_to_slots(rows)):
                part_out[half, 4 * group + member] = block
            return carry

        lax.fori_loop(0, n_vis // 4, pack_values, 0, unroll=8)
        send_all(
            lambda peer: part_out.at[half, peer],
            part_in.at[half],
            part_send.at[half],
            lambda step: part_recv.at[half],
        )
        part_in[half, me] = part_out[half, me]

    for load in loads[6:]:
        load.wait()
    wait_blocks(gain_all.at[core], n_vis // 2 - 1, gain_recv.at[0])
    to_other_core = pltpu.make_async_remote_copy(
        src_ref=gain_all.at[core],
        dst_ref=gain_all.at[core],
        send_sem=gain_send.at[1],
        recv_sem=gain_recv.at[1],
        device_id=(me ^ 1, facet),
        device_id_type=MESH,
    )
    to_other_core.start()
    wait_blocks(gain_all.at[1 - core], n_vis // 2, gain_recv.at[1])
    high, low = split_pair(gain_all[...].reshape(n_vis * 8, 256).T)
    both = jnp.concatenate([high, low], axis=0)
    interval = wide_row(interval_ref[...])
    holder = interval >> 2
    gain_row = ((holder & 1) * (n_vis // 2) + (holder >> 1)) * 8 + (interval & 3)
    station = lax.broadcasted_iota(jnp.int32, (64, slots), 0)
    at_p = jnp.where(station == wide_row(station_p_ref[...]), 1.0, 0.0)
    at_q = jnp.where(station == wide_row(station_q_ref[...]), 1.0, 0.0)
    index = lax.broadcasted_iota(jnp.int32, (n_vis * 8, slots), 0)
    jones_p = []
    jones_q = []
    for half in range(2):
        hot = jnp.where(index == gain_row + 4 * half, 1.0, 0.0).astype(BF16)
        picked = matmul(both, hot)
        picked = picked[:256] + picked[256:]
        for comp in range(4):
            here = picked[64 * comp : 64 * comp + 64]
            jones_p.append(jnp.sum(here * at_p, axis=0, keepdims=True))
            jones_q.append(jnp.sum(here * at_q, axis=0, keepdims=True))
    outer_re, outer_im = jones_outer(jones_p, jones_q)
    live = wide_row(live_ref[...]).astype(F32)
    scale = wide_row(weight_ref[...]) * live

    for half in range(2):
        here = slice(half * part, (half + 1) * part)
        wait_blocks(part_in.at[half], n_vis - 1, part_recv.at[half])
        model = jnp.sum(part_in[half], axis=0) * (1.0 / SIDE)
        model_re = wide_row(model[0:2])
        model_im = wide_row(model[2:4])
        own_re, own_im = outer_re[:, here], outer_im[:, here]
        pred_in[half, facet, 0:4, :] = model_re * own_re - model_im * own_im
        pred_in[half, facet, 4:8, :] = model_re * own_im + model_im * own_re

        for step in facet_steps:
            pltpu.make_async_remote_copy(
                src_ref=pred_in.at[half, facet],
                dst_ref=pred_in.at[half, facet],
                send_sem=pred_send.at[half],
                recv_sem=pred_recv.at[half],
                device_id=(me, facet_peer(step)),
                device_id_type=MESH,
            ).start()

    for half in range(2):
        here = slice(half * part, (half + 1) * part)
        wait_blocks(pred_in.at[half], n_facet - 1, pred_recv.at[half])
        predicted = pred_in[half, 0]
        for other in range(1, n_facet):
            predicted = predicted + pred_in[half, other]
        resid = (vis_ref[:, here] - predicted) * live[:, here]
        resid_ref[:, here] = resid
        stokes_re, stokes_im = jones_stokes(
            [gain[:, here] for gain in jones_p],
            [gain[:, here] for gain in jones_q],
            [resid[comp : comp + 1] for comp in range(8)],
        )
        stokes_in[half, me, 0:2, :] = tall_block(stokes_re * scale[:, here])
        stokes_in[half, me, 2:4, :] = tall_block(stokes_im * scale[:, here])
        send_all(
            lambda peer: stokes_in.at[half, me],
            stokes_in.at[half],
            stokes_send.at[half],
            lambda step: stokes_recv.at[half, step[0]],
        )

    def backward_pair(pair, place, first):
        total = jnp.zeros((4 * side_x, INNER), F32)
        half = pair // 8
        row = pl.ds(pair_row(pair), 1)
        whole_re = values[half, place, pl.ds(value_row(pair), 1), :]
        whole_im = values[half, place, pl.ds(value_row(pair) + 2, 1), :]
        whole_index = local_row[place, row, :]
        whole_cos = step_cos[place, row, :]
        whole_sin = step_sin[place, row, :]
        for start in range(0, width, chunk_w):
            lanes = slice(start, start + chunk_w)
            re = whole_re[:, lanes]
            im = whole_im[:, lanes]
            cos = fine_cos[pair, place, :, lanes]
            sin = fine_sin[pair, place, :, lanes]
            real_rows = [re * cos - im * sin]
            imag_rows = [re * sin + im * cos]
            cos = jnp.broadcast_to(whole_cos[:, lanes], (8, chunk_w))
            sin = jnp.broadcast_to(whole_sin[:, lanes], (8, chunk_w))
            for _ in range(blocks_x - 1):
                re, im = real_rows[-1], imag_rows[-1]
                real_rows.append(re * cos - im * sin)
                imag_rows.append(re * sin + im * cos)
            high, low = split_pair(jnp.concatenate(real_rows + imag_rows, axis=0))
            both = jnp.concatenate([high, low], axis=0)
            total = total + lax.dot_general(
                both,
                hot_columns(whole_index[:, lanes]),
                (((1,), (1,)), ((), ())),
                preferred_element_type=F32,
            )
        total = total[: 2 * side_x] + total[2 * side_x :]
        table[pair] = total if first else table[pair] + total

    for half in range(2):
        for away in range(2):
            place = side ^ away
            count = n_vis // 2 - (1 - away)
            wait_blocks(stokes_in.at[half], count, stokes_recv.at[half, away])

            def order_stokes(group, carry):
                lanes = pl.ds(pl.multiple_of(group * 128, 128), 128)
                first = place * (n_vis // 2) + 4 * group
                blocks = [stokes_in[half, first + member] for member in range(4)]
                for turn, rows in enumerate(slots_to_pairs(blocks)):
                    values[half, place, 4 * turn : 4 * turn + 4, lanes] = rows
                return carry

            def backward(pair, carry):
                backward_pair(pair, place, away == 0)
                return carry

            lax.fori_loop(0, n_vis // 8, order_stokes, 0, unroll=4)
            lax.fori_loop(8 * half, 8 * half + 8, backward, 0, unroll=8)

    wait_blocks(gain_all.at[core], n_vis // 2 - 1, gain_send.at[0])
    wait_blocks(gain_all.at[core], n_vis // 2, gain_send.at[1])
    for half in range(2):
        wait_blocks(part_in.at[half], n_vis - 1, part_send.at[half])
        wait_blocks(pred_in.at[half], n_facet - 1, pred_send.at[half])
        wait_blocks(stokes_in.at[half], n_vis - 1, stokes_send.at[half])


def image_kernel(
    factor,
    resid_ref,
    table,
    turn_ref,
    twist_ref,
    resid_hbm,
    dirty_hbm,
    work_re,
    work_im,
    lines,
    dirty,
    resid_sem,
    dirty_sem,
):
    side_x = dirty.shape[0]
    keep = pltpu.make_async_copy(resid_ref, resid_hbm, resid_sem)
    keep.start()

    def backward_rows(chunk, carry):
        rows = pl.ds(pl.multiple_of(chunk * 8, 8), 8)
        rows_im = pl.ds(pl.multiple_of(side_x + chunk * 8, 8), 8)
        vals = radix16([(table[q, rows, :], table[q, rows_im, :]) for q in range(RADIX)], 1.0)
        for b in range(RADIX):
            re, im = vals[b]
            cos = twist_ref[0, b : b + 1, :]
            sin = twist_ref[1, b : b + 1, :]
            work_re[b, rows, :] = re * cos - im * sin
            work_im[b, rows, :] = re * sin + im * cos
        return carry

    lax.fori_loop(0, side_x // 8, backward_rows, 0, unroll=8)

    last_hi = turn_ref[: 2 * INNER]
    last_lo = turn_ref[2 * INNER :]
    last_both = jnp.concatenate([last_hi, last_lo], axis=1)
    group_b = 8
    for start in range(0, RADIX, group_b):
        halves = [
            split_pair(jnp.concatenate([work_re[b], work_im[b]], axis=1))
            for b in range(start, start + group_b)
        ]
        high = jnp.concatenate([pair[0] for pair in halves], axis=0)
        low = jnp.concatenate([pair[1] for pair in halves], axis=0)
        both = matmul(high, last_both)
        part = (both[:, :INNER] + (both[:, INNER:] + matmul(low, last_hi))) * factor
        for place in range(group_b):
            here = part[place * side_x : (place + 1) * side_x]
            lines[pl.ds(start + place, INNER, stride=RADIX), :] = here.T
    count = dirty_sem.shape[0]
    wide = SIDE // count
    copies = []
    for piece in range(count):
        here = slice(piece * wide, (piece + 1) * wide)
        dirty[:, here] = lines[here, :].T
        copies.append(
            pltpu.make_async_copy(dirty.at[:, here], dirty_hbm.at[:, here], dirty_sem.at[piece])
        )
        copies[-1].start()
    for copy in copies:
        copy.wait()
    keep.wait()


def per_device(
    visibilities,
    weights,
    live_slots,
    station_p,
    station_q,
    interval,
    cell_row,
    cell_col,
    jones_gains,
    model_image,
):
    n_vis = lax.axis_size("vis")
    n_facet = lax.axis_size("facet")
    side_x = model_image.shape[1]
    slots = visibilities.shape[1]
    width = n_vis * slots // RADIX // 2

    def rows_of(array):
        return array.reshape(-1, 128)

    turn, twist = [jnp.asarray(table) for table in make_tables()]
    given = [
        visibilities,
        rows_of(weights),
        rows_of(live_slots),
        rows_of(station_p),
        rows_of(station_q),
        rows_of(interval),
        rows_of(cell_row),
        rows_of(cell_col),
        jones_gains[0],
        model_image[0],
        turn,
        twist,
    ]
    in_hbm = pl.BlockSpec(memory_space=pltpu.HBM)
    in_vmem = pl.BlockSpec(memory_space=pltpu.VMEM)
    work = pltpu.VMEM((RADIX, side_x, INNER), F32)
    kept = pl.pallas_call(
        functools.partial(exchange_kernel, n_vis, n_facet),
        out_shape=(
            pltpu.VMEM((8, slots), F32),
            pltpu.VMEM((RADIX, 2 * side_x, INNER), F32),
            pltpu.VMEM(turn.shape, turn.dtype),
            pltpu.VMEM(twist.shape, twist.dtype),
        ),
        in_specs=[in_hbm] * len(given),
        out_specs=(in_vmem,) * 4,
        scratch_shapes=[pltpu.VMEM(array.shape, array.dtype) for array in given[:-2]]
        + [
            pltpu.VMEM((2, n_vis // 2, 8, 256), F32),
            pltpu.VMEM((2, n_vis, 4, 128), F32),
            pltpu.VMEM((2, n_vis, 4, 128), F32),
            pltpu.VMEM((2, n_facet, 8, slots // 2), F32),
            pltpu.VMEM((2, n_vis, 4, 128), F32),
            pltpu.VMEM((SIDE, side_x), F32),
            work,
            work,
            pltpu.VMEM((2, 16, width), jnp.int32),
            pltpu.VMEM((2, 16, width), jnp.int32),
            pltpu.VMEM((2, 2, 16, width), F32),
            pltpu.VMEM((2, 16, width), F32),
            pltpu.VMEM((2, 16, width), F32),
            pltpu.VMEM((RADIX, 2, 8, width), F32),
            pltpu.VMEM((RADIX, 2, 8, width), F32),
            pltpu.SemaphoreType.DMA((len(given),)),
        ]
        + [pltpu.SemaphoreType.DMA((2,))] * 7
        + [pltpu.SemaphoreType.DMA((2, 2))],
        compiler_params=pltpu.CompilerParams(
            collective_id=0, has_side_effects=True, vmem_limit_bytes=40 * 1024 * 1024
        ),
    )(*[pltpu.with_memory_space_constraint(array, pltpu.HBM) for array in given])
    resid, dirty = pl.pallas_call(
        functools.partial(image_kernel, 4.0 / math.sqrt(slots * n_vis)),
        out_shape=(
            pltpu.HBM((8, slots), F32),
            pltpu.HBM((side_x, SIDE), F32),
        ),
        in_specs=[in_vmem] * 4,
        out_specs=(in_hbm, in_hbm),
        scratch_shapes=[
            work,
            work,
            pltpu.VMEM((SIDE, side_x), F32),
            pltpu.VMEM((side_x, SIDE), F32),
            pltpu.SemaphoreType.DMA(()),
            pltpu.SemaphoreType.DMA((4,)),
        ],
        compiler_params=pltpu.CompilerParams(vmem_limit_bytes=40 * 1024 * 1024),
    )(*kept)
    return resid, dirty[None]


def solution(mesh):
    return jax.shard_map(
        per_device,
        mesh=mesh,
        in_specs=(
            P(None, "vis"),
            P("vis"),
            P("vis"),
            P("vis"),
            P("vis"),
            P("vis"),
            P(),
            P(),
            P("facet", None, "vis", None),
            P("facet", "vis", None),
        ),
        out_specs=(P(None, "vis"), P("facet", "vis", None)),
        check_vma=False,
    )
```

```python
import functools
import math

import jax
import jax.numpy as jnp
import numpy as np
from jax import lax
from jax.experimental import pallas as pl
from jax.experimental.pallas import tpu as pltpu
from jax.sharding import PartitionSpec as P

TWO_PI = 2.0 * math.pi
MESH = pl.DeviceIdType.MESH
F32 = jnp.float32
BF16 = jnp.bfloat16

RADIX = 16
INNER = 128
SIDE = RADIX * INNER
PARTS = 2


def split_table(table):
    high = table.astype(BF16)
    low = (table - high.astype(np.float64)).astype(BF16)
    return high, low


def make_tables():
    inner = np.arange(INNER)
    angle = TWO_PI * (np.outer(inner, inner) % INNER) / INNER
    turn = np.concatenate([np.cos(angle), -np.sin(angle)], axis=0)
    twist = TWO_PI * np.outer(np.arange(RADIX), inner) / SIDE
    twist = np.stack([np.cos(twist), np.sin(twist)]).astype(np.float32)
    return np.concatenate(split_table(turn), axis=0), twist


def split_pair(value):
    high = value.astype(BF16)
    low = (value - high.astype(F32)).astype(BF16)
    return high, low


def matmul(left, right):
    return jnp.dot(left, right, preferred_element_type=F32)


def cmul_const(pair, real, imag):
    re, im = pair
    return re * real - im * imag, re * imag + im * real


def radix4(vals, sign):
    (ar, ai), (br, bi), (cr, ci), (dr, di) = vals
    sr, si = ar + cr, ai + ci
    tr, ti = ar - cr, ai - ci
    ur, ui = br + dr, bi + di
    wr, wi = br - dr, bi - di
    if sign < 0:
        xr, xi = wi, -wr
    else:
        xr, xi = -wi, wr
    return [(sr + ur, si + ui), (tr + xr, ti + xi), (sr - ur, si - ui), (tr - xr, ti - xi)]


def radix16(vals, sign):
    inner = [radix4([vals[4 * n1 + n2] for n1 in range(4)], sign) for n2 in range(4)]
    out = [None] * 16
    for k1 in range(4):
        column = []
        for n2 in range(4):
            turn = n2 * k1
            value = inner[n2][k1]
            if turn == 4:
                re, im = value
                value = (im, -re) if sign < 0 else (-im, re)
            elif turn == 2 or turn == 6:
                half = math.sqrt(0.5)
                re, im = value
                if sign < 0:
                    value = ((re + im) * half, (im - re) * half)
                else:
                    value = ((re - im) * half, (re + im) * half)
                if turn == 6:
                    re, im = value
                    value = (im, -re) if sign < 0 else (-im, re)
            elif turn:
                angle = sign * TWO_PI * turn / 16
                value = cmul_const(value, math.cos(angle), math.sin(angle))
            column.append(value)
        for k2, value in enumerate(radix4(column, sign)):
            out[k1 + 4 * k2] = value
    return out


def unit_phase(step):
    quarter = (step + 256) >> 9
    angle = (step - (quarter << 9)).astype(F32) * (TWO_PI / SIDE)
    square = angle * angle
    sine = angle * (
        1.0
        + square
        * (-1.6666654611e-1 + square * (8.3321608736e-3 + square * -1.9515295891e-4))
    )
    cosine = 1.0 + square * (
        -0.5
        + square
        * (4.166664568298827e-2 + square * (-1.388731625493765e-3 + square * 2.443315711809948e-5))
    )
    odd = (quarter & 1) == 1
    cos_mag = jnp.where(odd, sine, cosine)
    sin_mag = jnp.where(odd, cosine, sine)
    cos_val = jnp.where(((quarter + 1) & 2) == 2, -cos_mag, cos_mag)
    sin_val = jnp.where((quarter & 2) == 2, -sin_mag, sin_mag)
    return cos_val, sin_val


def pick_lanes(value, index):
    numbers = lax.GatherDimensionNumbers(
        offset_dims=(),
        collapsed_slice_dims=(1,),
        start_index_map=(1,),
        operand_batching_dims=(0,),
        start_indices_batching_dims=(0,),
    )
    return lax.gather(
        value,
        index[..., None],
        numbers,
        slice_sizes=(1, 1),
        mode=lax.GatherScatterMode.PROMISE_IN_BOUNDS,
    )


def lane_block(shape):
    return lax.broadcasted_iota(jnp.int32, shape, 1) >> 5


def slots_to_pairs(blocks):
    where = lane_block(blocks[0].shape)
    rows = []
    for turn in range(4):
        total = None
        for member in range(4):
            shift = 32 * (member - turn) % 128
            moved = pltpu.roll(blocks[member], shift, 1) if shift else blocks[member]
            total = moved if total is None else jnp.where(where == member, moved, total)
        rows.append(total)
    return rows


def pairs_to_slots(rows):
    where = lane_block(rows[0].shape)
    blocks = []
    for member in range(4):
        total = None
        for turn in range(4):
            shift = 32 * (turn - member) % 128
            moved = pltpu.roll(rows[turn], shift, 1) if shift else rows[turn]
            total = moved if total is None else jnp.where(where == turn, moved, total)
        blocks.append(total)
    return blocks


def wide_row(block):
    return jnp.concatenate([block[k : k + 1, :] for k in range(block.shape[0])], axis=1)


def tall_block(row):
    count = row.shape[1] // 128
    return jnp.concatenate([row[:, 128 * k : 128 * (k + 1)] for k in range(count)], axis=0)


def jones_outer(left, right):
    real_rows = []
    imag_rows = []
    for row_a in range(2):
        for row_b in range(2):
            real_sum = 0.0
            imag_sum = 0.0
            for inner in range(2):
                left_re = left[row_a * 2 + inner]
                left_im = left[4 + row_a * 2 + inner]
                right_re = right[row_b * 2 + inner]
                right_im = right[4 + row_b * 2 + inner]
                real_sum = real_sum + left_re * right_re + left_im * right_im
                imag_sum = imag_sum + left_im * right_re - left_re * right_im
            real_rows.append(real_sum)
            imag_rows.append(imag_sum)
    return jnp.concatenate(real_rows, axis=0), jnp.concatenate(imag_rows, axis=0)


def jones_stokes(left, right, resid):
    total_re = 0.0
    total_im = 0.0
    for inner in range(2):
        for row_a in range(2):
            for row_b in range(2):
                left_re = left[row_a * 2 + inner]
                left_im = left[4 + row_a * 2 + inner]
                res_re = resid[row_a * 2 + row_b]
                res_im = resid[4 + row_a * 2 + row_b]
                right_re = right[row_b * 2 + inner]
                right_im = right[4 + row_b * 2 + inner]
                mid_re = left_re * res_re + left_im * res_im
                mid_im = left_re * res_im - left_im * res_re
                total_re = total_re + mid_re * right_re - mid_im * right_im
                total_im = total_im + mid_re * right_im + mid_im * right_re
    return 0.5 * total_re, 0.5 * total_im


def exchange_kernel(
    n_vis,
    n_facet,
    vis_hbm,
    weight_hbm,
    live_hbm,
    station_p_hbm,
    station_q_hbm,
    interval_hbm,
    cell_row_hbm,
    cell_col_hbm,
    gain_hbm,
    image_hbm,
    turn_hbm,
    twist_hbm,
    resid_ref,
    table,
    turn_ref,
    twist_ref,
    vis_ref,
    weight_ref,
    live_ref,
    station_p_ref,
    station_q_ref,
    interval_ref,
    cell_row_ref,
    cell_col_ref,
    gain_ref,
    image_ref,
    gain_all,
    part_out,
    part_in,
    pred_in,
    stokes_in,
    lines,
    work_re,
    work_im,
    local_row,
    local_col,
    values,
    step_cos,
    step_sin,
    fine_cos,
    fine_sin,
    load_sem,
    gain_send,
    gain_recv,
    gain_pair_send,
    gain_pair_recv,
    part_send,
    part_recv,
    pred_send,
    pred_recv,
    stokes_send,
    stokes_recv,
):
    me = lax.axis_index("vis")
    facet = lax.axis_index("facet")
    side_x = image_ref.shape[0]
    width = values.shape[3]
    slots = vis_ref.shape[1]
    parts, rows_k = part_in.shape[0], part_in.shape[2] // 2
    part = slots // parts
    part_pairs = RADIX // parts

    order = (
        (cell_row_hbm, cell_row_ref),
        (cell_col_hbm, cell_col_ref),
        (gain_hbm, gain_ref),
        (image_hbm, image_ref),
        (turn_hbm, turn_ref),
        (twist_hbm, twist_ref),
        (interval_hbm, interval_ref),
        (station_p_hbm, station_p_ref),
        (station_q_hbm, station_q_ref),
        (live_hbm, live_ref),
        (weight_hbm, weight_ref),
        (vis_hbm, vis_ref),
    )
    loads = [
        pltpu.make_async_copy(source, target, load_sem.at[place])
        for place, (source, target) in enumerate(order)
    ]
    for load in loads:
        load.start()

    ring_z, ring_y = n_vis // 4, n_facet // 2
    side = me // (2 * ring_z)
    vis_steps = [
        (away, along, core)
        for away in range(2)
        for along in range(ring_z)
        for core in range(2)
        if (away, along, core) != (0, 0, 0)
    ]
    vis_steps.sort(key=lambda step: (-2 * step[0] - min(step[1], ring_z - step[1]), -step[2]))
    facet_steps = [(along, away) for along in range(ring_y) for away in range(2) if along or away]
    facet_steps.sort(key=lambda step: -min(step[0], ring_y - step[0]) - step[1])

    def vis_peer(step):
        away, along, core = step
        z = lax.rem(me // 2 + along, ring_z)
        return ((side ^ away) * ring_z + z) * 2 + ((me & 1) ^ core)

    def facet_peer(step):
        along, away = step
        return lax.rem(facet // 2 + along, ring_y) * 2 + ((facet & 1) ^ away)

    barrier = pltpu.get_barrier_semaphore()
    for step in vis_steps:
        pl.semaphore_signal(barrier, 1, device_id=(vis_peer(step), facet), device_id_type=MESH)
    for step in facet_steps:
        pl.semaphore_signal(barrier, 1, device_id=(me, facet_peer(step)), device_id_type=MESH)

    def send_all(source, target, send_sem, recv_sem):
        for step in vis_steps:
            peer = vis_peer(step)
            pltpu.make_async_remote_copy(
                src_ref=source(peer),
                dst_ref=target.at[me],
                send_sem=send_sem,
                recv_sem=recv_sem(step),
                device_id=(peer, facet),
                device_id_type=MESH,
            ).start()

    def wait_blocks(buffer, count, sem):
        view = buffer.at[pl.ds(0, count)]
        pltpu.make_async_copy(view, view, sem).wait()

    def pair_row(pair):
        return lax.rem(pair, 4) * 4 + pair // 4

    loads[0].wait()
    loads[1].wait()

    def group_place(group):
        return group // 4, pl.ds(pl.multiple_of(lax.rem(group, 4) * 128, 128), 128)

    def order_cells(group, carry):
        place, lanes = group_place(group)

        def read(holder):
            rows = pl.ds(holder * 4, 4)
            return jnp.concatenate([cell_row_ref[rows, :], cell_col_ref[rows, :]], axis=0)

        for turn, rows in enumerate(slots_to_pairs([read(4 * group + k) for k in range(4)])):
            lane = lax.broadcasted_iota(jnp.int32, (4, 128), 1)
            local_row[place, 4 * turn : 4 * turn + 4, lanes] = rows[0:4] + ((lane >> 4) & 1) * 64
            local_col[place, 4 * turn : 4 * turn + 4, lanes] = rows[4:8]
        return carry

    lax.fori_loop(0, n_vis // 4, order_cells, 0, unroll=4)
    for place in range(2):
        cos, sin = unit_phase((local_col[place] * 8) & (SIDE - 1))
        step_cos[place] = cos
        step_sin[place] = sin

    loads[2].wait()
    intervals_here = gain_ref.shape[1]
    stations = gain_ref.shape[2]
    core, chip = me & 1, me // 2
    gain_all[core, chip] = jnp.zeros((8, 256), F32)
    for comp in range(8):
        half, lane = comp // 4, 64 * (comp % 4)
        rows = slice(4 * half, 4 * half + intervals_here)
        gain_all[core, chip, rows, lane : lane + stations] = gain_ref[comp]

    loads[3].wait()
    lines[...] = image_ref[...].T
    loads[4].wait()
    loads[5].wait()
    first_hi = jnp.concatenate([turn_ref[:INNER], turn_ref[INNER : 2 * INNER]], axis=1)
    first_lo = jnp.concatenate([turn_ref[2 * INNER : 3 * INNER], turn_ref[3 * INNER :]], axis=1)
    first_twice = jnp.concatenate([first_hi, first_hi], axis=0)
    group_b = 8
    for start in range(0, RADIX, group_b):
        halves = [
            split_pair(lines[pl.ds(b, INNER, stride=RADIX), :].T)
            for b in range(start, start + group_b)
        ]
        high = jnp.concatenate([pair[0] for pair in halves], axis=0)
        low = jnp.concatenate([pair[1] for pair in halves], axis=0)
        both = matmul(jnp.concatenate([high, low], axis=1), first_twice) + matmul(high, first_lo)
        for place in range(group_b):
            b = start + place
            here = both[place * side_x : (place + 1) * side_x]
            re, im = here[:, :INNER], here[:, INNER:]
            cos = twist_ref[0, b : b + 1, :]
            sin = twist_ref[1, b : b + 1, :]
            work_re[b] = re * cos + im * sin
            work_im[b] = im * cos - re * sin

    def forward_rows(chunk, carry):
        rows = pl.ds(pl.multiple_of(chunk * 8, 8), 8)
        rows_im = pl.ds(pl.multiple_of(side_x + chunk * 8, 8), 8)
        vals = radix16([(work_re[b, rows, :], work_im[b, rows, :]) for b in range(RADIX)], -1.0)
        for q in range(RADIX):
            table[q, rows, :] = vals[q][0]
            table[q, rows_im, :] = vals[q][1]
        return carry

    lax.fori_loop(0, side_x // 8, forward_rows, 0, unroll=4)

    pl.semaphore_wait(barrier, n_vis + n_facet - 2)
    for step in vis_steps:
        if step[2] == 0:
            pltpu.make_async_remote_copy(
                src_ref=gain_all.at[core, chip],
                dst_ref=gain_all.at[core, chip],
                send_sem=gain_send.at[0],
                recv_sem=gain_recv.at[step[0]],
                device_id=(vis_peer(step), facet),
                device_id_type=MESH,
            ).start()

    chunk_w = 256
    by_lanes = 256
    blocks_x = side_x // 8

    def hot_columns(local):
        index = lax.broadcasted_iota(jnp.int32, (INNER, local.shape[1]), 0)
        return jnp.where(index == local, 1.0, 0.0).astype(BF16)

    def value_row(pair):
        return lax.rem(pair, 4) * 2 * rows_k + lax.rem(pair // 4, rows_k)

    def forward_pair(pair, carry):
        half = pair // part_pairs
        row = pl.ds(pair_row(pair), 1)
        high, low = split_pair(table[pair])
        both = jnp.concatenate([high, low], axis=0)

        def picked_by_matmul(local):
            picked = matmul(both, hot_columns(local))
            picked = picked[: 2 * side_x] + picked[2 * side_x :]
            return lambda first: picked[first : first + 8]

        def picked_by_lanes(local):
            index = jnp.broadcast_to(local, (8, INNER))
            return lambda first: pick_lanes(table[pair, first : first + 8, :], index)

        pieces = [(start, INNER, picked_by_lanes) for start in range(0, by_lanes, INNER)]
        pieces += [(start, 256, picked_by_matmul) for start in range(by_lanes, width, 256)]
        for place in range(2):
            out_re = []
            out_im = []
            whole_index = local_row[place, row, :]
            whole_cos = step_cos[place, row, :]
            whole_sin = step_sin[place, row, :]
            x_index = me * side_x + lax.broadcasted_iota(jnp.int32, (8, width), 0)
            all_cos, all_sin = unit_phase((local_col[place, row, :] * x_index) & (SIDE - 1))
            fine_cos[pair, place] = all_cos
            fine_sin[pair, place] = all_sin
            for start, size, picker in pieces:
                lanes = slice(start, start + size)
                pick = picker(whole_index[:, lanes])
                cos = jnp.broadcast_to(whole_cos[:, lanes], (8, size))
                sin = jnp.broadcast_to(whole_sin[:, lanes], (8, size))
                sum_re = pick(8 * blocks_x - 8)
                sum_im = pick(side_x + 8 * blocks_x - 8)
                for block in range(blocks_x - 2, -1, -1):
                    re = pick(8 * block)
                    im = pick(side_x + 8 * block)
                    sum_re, sum_im = (
                        re + (sum_re * cos + sum_im * sin),
                        im + (sum_im * cos - sum_re * sin),
                    )
                cos = all_cos[:, lanes]
                sin = all_sin[:, lanes]
                out_re.append(jnp.sum(sum_re * cos + sum_im * sin, axis=0, keepdims=True))
                out_im.append(jnp.sum(sum_im * cos - sum_re * sin, axis=0, keepdims=True))
            re_row = pl.ds(value_row(pair), 1)
            im_row = pl.ds(value_row(pair) + rows_k, 1)
            values[half, place, re_row, :] = jnp.concatenate(out_re, axis=1)
            values[half, place, im_row, :] = jnp.concatenate(out_im, axis=1)
        return carry

    for half in range(parts):
        lax.fori_loop(
            part_pairs * half, part_pairs * (half + 1), forward_pair, 0, unroll=min(8, part_pairs)
        )

        def pack_values(group, carry):
            place, lanes = group_place(group)
            rows = [
                values[half, place, 2 * rows_k * turn : 2 * rows_k * (turn + 1), lanes]
                for turn in range(4)
            ]
            for member, block in enumerate(pairs_to_slots(rows)):
                part_out[half, 4 * group + member] = block
            return carry

        lax.fori_loop(0, n_vis // 4, pack_values, 0, unroll=8)
        send_all(
            lambda peer: part_out.at[half, peer],
            part_in.at[half],
            part_send.at[half],
            lambda step: part_recv.at[half],
        )
        part_in[half, me] = part_out[half, me]

    for load in loads[6:]:
        load.wait()
    interval = wide_row(interval_ref[...])
    holder = interval >> 2
    gain_row = ((holder & 1) * (n_vis // 2) + (holder >> 1)) * 8 + (interval & 3)
    station = lax.broadcasted_iota(jnp.int32, (64, slots), 0)
    at_p = jnp.where(station == wide_row(station_p_ref[...]), 1.0, 0.0)
    at_q = jnp.where(station == wide_row(station_q_ref[...]), 1.0, 0.0)
    index = lax.broadcasted_iota(jnp.int32, (n_vis * 8, slots), 0)
    hots = [
        jnp.where(index == gain_row + 4 * half, 1.0, 0.0).astype(BF16) for half in range(2)
    ]
    live = wide_row(live_ref[...]).astype(F32)
    scale = wide_row(weight_ref[...]) * live
    to_other_core = []
    for away in range(2):
        wait_blocks(gain_all.at[core], ring_z - 1 + away, gain_recv.at[away])
        chips = pl.ds((side ^ away) * ring_z, ring_z)
        to_other_core.append(
            pltpu.make_async_remote_copy(
                src_ref=gain_all.at[core, chips],
                dst_ref=gain_all.at[core, chips],
                send_sem=gain_pair_send.at[away],
                recv_sem=gain_pair_recv.at[away],
                device_id=(me ^ 1, facet),
                device_id_type=MESH,
            )
        )
        to_other_core[-1].start()
    for away in range(2):
        wait_blocks(gain_all.at[1 - core], ring_z, gain_pair_recv.at[away])
    high, low = split_pair(gain_all[...].reshape(n_vis * 8, 256).T)
    both = jnp.concatenate([high, low], axis=0)
    jones_p = []
    jones_q = []
    for half in range(2):
        picked = matmul(both, hots[half])
        picked = picked[:256] + picked[256:]
        for comp in range(4):
            here = picked[64 * comp : 64 * comp + 64]
            jones_p.append(jnp.sum(here * at_p, axis=0, keepdims=True))
            jones_q.append(jnp.sum(here * at_q, axis=0, keepdims=True))
    outer_re, outer_im = jones_outer(jones_p, jones_q)

    for half in range(parts):
        here = slice(half * part, (half + 1) * part)
        wait_blocks(part_in.at[half], n_vis - 1, part_recv.at[half])
        model = jnp.sum(part_in[half], axis=0) * (1.0 / SIDE)
        model_re = wide_row(model[:rows_k])
        model_im = wide_row(model[rows_k:])
        own_re, own_im = outer_re[:, here], outer_im[:, here]
        pred_in[half, facet, 0:4, :] = model_re * own_re - model_im * own_im
        pred_in[half, facet, 4:8, :] = model_re * own_im + model_im * own_re

        for step in facet_steps:
            pltpu.make_async_remote_copy(
                src_ref=pred_in.at[half, facet],
                dst_ref=pred_in.at[half, facet],
                send_sem=pred_send.at[half],
                recv_sem=pred_recv.at[half],
                device_id=(me, facet_peer(step)),
                device_id_type=MESH,
            ).start()

    for half in range(parts):
        here = slice(half * part, (half + 1) * part)
        wait_blocks(pred_in.at[half], n_facet - 1, pred_recv.at[half])
        predicted = pred_in[half, 0]
        for other in range(1, n_facet):
            predicted = predicted + pred_in[half, other]
        resid = (vis_ref[:, here] - predicted) * live[:, here]
        resid_ref[:, here] = resid
        stokes_re, stokes_im = jones_stokes(
            [gain[:, here] for gain in jones_p],
            [gain[:, here] for gain in jones_q],
            [resid[comp : comp + 1] for comp in range(8)],
        )
        stokes_in[half, me, :rows_k, :] = tall_block(stokes_re * scale[:, here])
        stokes_in[half, me, rows_k:, :] = tall_block(stokes_im * scale[:, here])
        send_all(
            lambda peer: stokes_in.at[half, me],
            stokes_in.at[half],
            stokes_send.at[half],
            lambda step: stokes_recv.at[half, step[0]],
        )

    def backward_pair(pair, place, first):
        total = jnp.zeros((4 * side_x, INNER), F32)
        half = pair // part_pairs
        row = pl.ds(pair_row(pair), 1)
        whole_re = values[half, place, pl.ds(value_row(pair), 1), :]
        whole_im = values[half, place, pl.ds(value_row(pair) + rows_k, 1), :]
        whole_index = local_row[place, row, :]
        whole_cos = step_cos[place, row, :]
        whole_sin = step_sin[place, row, :]
        for start in range(0, width, chunk_w):
            lanes = slice(start, start + chunk_w)
            re = whole_re[:, lanes]
            im = whole_im[:, lanes]
            cos = fine_cos[pair, place, :, lanes]
            sin = fine_sin[pair, place, :, lanes]
            real_rows = [re * cos - im * sin]
            imag_rows = [re * sin + im * cos]
            cos = jnp.broadcast_to(whole_cos[:, lanes], (8, chunk_w))
            sin = jnp.broadcast_to(whole_sin[:, lanes], (8, chunk_w))
            for _ in range(blocks_x - 1):
                re, im = real_rows[-1], imag_rows[-1]
                real_rows.append(re * cos - im * sin)
                imag_rows.append(re * sin + im * cos)
            high, low = split_pair(jnp.concatenate(real_rows + imag_rows, axis=0))
            both = jnp.concatenate([high, low], axis=0)
            total = total + lax.dot_general(
                both,
                hot_columns(whole_index[:, lanes]),
                (((1,), (1,)), ((), ())),
                preferred_element_type=F32,
            )
        total = total[: 2 * side_x] + total[2 * side_x :]
        table[pair] = total if first else table[pair] + total

    for half in range(parts):
        for away in range(2):
            place = side ^ away
            count = n_vis // 2 - (1 - away)
            wait_blocks(stokes_in.at[half], count, stokes_recv.at[half, away])

            def order_stokes(group, carry):
                lanes = pl.ds(pl.multiple_of(group * 128, 128), 128)
                first = place * (n_vis // 2) + 4 * group
                blocks = [stokes_in[half, first + member] for member in range(4)]
                for turn, rows in enumerate(slots_to_pairs(blocks)):
                    values[half, place, 2 * rows_k * turn : 2 * rows_k * (turn + 1), lanes] = rows
                return carry

            def backward(pair, carry):
                backward_pair(pair, place, away == 0)
                return carry

            lax.fori_loop(0, n_vis // 8, order_stokes, 0, unroll=4)
            lax.fori_loop(
                part_pairs * half, part_pairs * (half + 1), backward, 0, unroll=min(8, part_pairs)
            )

    wait_blocks(gain_all.at[core], n_vis // 2 - 1, gain_send.at[0])
    for away in range(2):
        wait_blocks(gain_all.at[core], ring_z, gain_pair_send.at[away])
    for half in range(parts):
        wait_blocks(part_in.at[half], n_vis - 1, part_send.at[half])
        wait_blocks(pred_in.at[half], n_facet - 1, pred_send.at[half])
        wait_blocks(stokes_in.at[half], n_vis - 1, stokes_send.at[half])


def image_kernel(
    factor,
    resid_ref,
    table,
    turn_ref,
    twist_ref,
    resid_hbm,
    dirty_hbm,
    work_re,
    work_im,
    lines,
    dirty,
    resid_sem,
    dirty_sem,
):
    side_x = dirty.shape[0]
    keep = pltpu.make_async_copy(resid_ref, resid_hbm, resid_sem)
    keep.start()

    def backward_rows(chunk, carry):
        rows = pl.ds(pl.multiple_of(chunk * 8, 8), 8)
        rows_im = pl.ds(pl.multiple_of(side_x + chunk * 8, 8), 8)
        vals = radix16([(table[q, rows, :], table[q, rows_im, :]) for q in range(RADIX)], 1.0)
        for b in range(RADIX):
            re, im = vals[b]
            cos = twist_ref[0, b : b + 1, :]
            sin = twist_ref[1, b : b + 1, :]
            work_re[b, rows, :] = re * cos - im * sin
            work_im[b, rows, :] = re * sin + im * cos
        return carry

    lax.fori_loop(0, side_x // 8, backward_rows, 0, unroll=8)

    last_hi = turn_ref[: 2 * INNER]
    last_lo = turn_ref[2 * INNER :]
    last_both = jnp.concatenate([last_hi, last_lo], axis=1)
    group_b = 8
    for start in range(0, RADIX, group_b):
        halves = [
            split_pair(jnp.concatenate([work_re[b], work_im[b]], axis=1))
            for b in range(start, start + group_b)
        ]
        high = jnp.concatenate([pair[0] for pair in halves], axis=0)
        low = jnp.concatenate([pair[1] for pair in halves], axis=0)
        both = matmul(high, last_both)
        part = (both[:, :INNER] + (both[:, INNER:] + matmul(low, last_hi))) * factor
        for place in range(group_b):
            here = part[place * side_x : (place + 1) * side_x]
            lines[pl.ds(start + place, INNER, stride=RADIX), :] = here.T
    count = dirty_sem.shape[0]
    wide = SIDE // count
    copies = []
    for piece in range(count):
        here = slice(piece * wide, (piece + 1) * wide)
        dirty[:, here] = lines[here, :].T
        copies.append(
            pltpu.make_async_copy(dirty.at[:, here], dirty_hbm.at[:, here], dirty_sem.at[piece])
        )
        copies[-1].start()
    for copy in copies:
        copy.wait()
    keep.wait()


def per_device(
    visibilities,
    weights,
    live_slots,
    station_p,
    station_q,
    interval,
    cell_row,
    cell_col,
    jones_gains,
    model_image,
):
    n_vis = lax.axis_size("vis")
    n_facet = lax.axis_size("facet")
    side_x = model_image.shape[1]
    slots = visibilities.shape[1]
    width = n_vis * slots // RADIX // 2

    def rows_of(array):
        return array.reshape(-1, 128)

    turn, twist = [jnp.asarray(table) for table in make_tables()]
    given = [
        visibilities,
        rows_of(weights),
        rows_of(live_slots),
        rows_of(station_p),
        rows_of(station_q),
        rows_of(interval),
        rows_of(cell_row),
        rows_of(cell_col),
        jones_gains[0],
        model_image[0],
        turn,
        twist,
    ]
    in_hbm = pl.BlockSpec(memory_space=pltpu.HBM)
    in_vmem = pl.BlockSpec(memory_space=pltpu.VMEM)
    work = pltpu.VMEM((RADIX, side_x, INNER), F32)
    kept = pl.pallas_call(
        functools.partial(exchange_kernel, n_vis, n_facet),
        out_shape=(
            pltpu.VMEM((8, slots), F32),
            pltpu.VMEM((RADIX, 2 * side_x, INNER), F32),
            pltpu.VMEM(turn.shape, turn.dtype),
            pltpu.VMEM(twist.shape, twist.dtype),
        ),
        in_specs=[in_hbm] * len(given),
        out_specs=(in_vmem,) * 4,
        scratch_shapes=[pltpu.VMEM(array.shape, array.dtype) for array in given[:-2]]
        + [
            pltpu.VMEM((2, n_vis // 2, 8, 256), F32),
            pltpu.VMEM((PARTS, n_vis, 8 // PARTS, 128), F32),
            pltpu.VMEM((PARTS, n_vis, 8 // PARTS, 128), F32),
            pltpu.VMEM((PARTS, n_facet, 8, slots // PARTS), F32),
            pltpu.VMEM((PARTS, n_vis, 8 // PARTS, 128), F32),
            pltpu.VMEM((SIDE, side_x), F32),
            work,
            work,
            pltpu.VMEM((2, 16, width), jnp.int32),
            pltpu.VMEM((2, 16, width), jnp.int32),
            pltpu.VMEM((PARTS, 2, 32 // PARTS, width), F32),
            pltpu.VMEM((2, 16, width), F32),
            pltpu.VMEM((2, 16, width), F32),
            pltpu.VMEM((RADIX, 2, 8, width), F32),
            pltpu.VMEM((RADIX, 2, 8, width), F32),
            pltpu.SemaphoreType.DMA((len(given),)),
        ]
        + [pltpu.SemaphoreType.DMA((2,))] * 4
        + [pltpu.SemaphoreType.DMA((PARTS,))] * 5
        + [pltpu.SemaphoreType.DMA((PARTS, 2))],
        compiler_params=pltpu.CompilerParams(
            collective_id=0, has_side_effects=True, vmem_limit_bytes=40 * 1024 * 1024
        ),
    )(*[pltpu.with_memory_space_constraint(array, pltpu.HBM) for array in given])
    resid, dirty = pl.pallas_call(
        functools.partial(image_kernel, 4.0 / math.sqrt(slots * n_vis)),
        out_shape=(
            pltpu.HBM((8, slots), F32),
            pltpu.HBM((side_x, SIDE), F32),
        ),
        in_specs=[in_vmem] * 4,
        out_specs=(in_hbm, in_hbm),
        scratch_shapes=[
            work,
            work,
            pltpu.VMEM((SIDE, side_x), F32),
            pltpu.VMEM((side_x, SIDE), F32),
            pltpu.SemaphoreType.DMA(()),
            pltpu.SemaphoreType.DMA((4,)),
        ],
        compiler_params=pltpu.CompilerParams(vmem_limit_bytes=40 * 1024 * 1024),
    )(*kept)
    return resid, dirty[None]


def solution(mesh):
    return jax.shard_map(
        per_device,
        mesh=mesh,
        in_specs=(
            P(None, "vis"),
            P("vis"),
            P("vis"),
            P("vis"),
            P("vis"),
            P("vis"),
            P(),
            P(),
            P("facet", None, "vis", None),
            P("facet", "vis", None),
        ),
        out_specs=(P(None, "vis"), P("facet", "vis", None)),
        check_vma=False,
    )
```

```python
import functools
import math

import jax
import jax.numpy as jnp
import numpy as np
from jax import lax
from jax.experimental import pallas as pl
from jax.experimental.pallas import tpu as pltpu
from jax.sharding import PartitionSpec as P

TWO_PI = 2.0 * math.pi
MESH = pl.DeviceIdType.MESH
F32 = jnp.float32
BF16 = jnp.bfloat16

RADIX = 16
INNER = 128
SIDE = RADIX * INNER
PARTS = 2


def split_table(table):
    high = table.astype(BF16)
    low = (table - high.astype(np.float64)).astype(BF16)
    return high, low


def make_tables():
    inner = np.arange(INNER)
    angle = TWO_PI * (np.outer(inner, inner) % INNER) / INNER
    turn = np.concatenate([np.cos(angle), -np.sin(angle)], axis=0)
    twist = TWO_PI * np.outer(np.arange(RADIX), inner) / SIDE
    twist = np.stack([np.cos(twist), np.sin(twist)]).astype(np.float32)
    return np.concatenate(split_table(turn), axis=0), twist


def split_pair(value):
    high = value.astype(BF16)
    low = (value - high.astype(F32)).astype(BF16)
    return high, low


def matmul(left, right):
    return jnp.dot(left, right, preferred_element_type=F32)


def cmul_const(pair, real, imag):
    re, im = pair
    return re * real - im * imag, re * imag + im * real


def radix4(vals, sign):
    (ar, ai), (br, bi), (cr, ci), (dr, di) = vals
    sr, si = ar + cr, ai + ci
    tr, ti = ar - cr, ai - ci
    ur, ui = br + dr, bi + di
    wr, wi = br - dr, bi - di
    if sign < 0:
        xr, xi = wi, -wr
    else:
        xr, xi = -wi, wr
    return [(sr + ur, si + ui), (tr + xr, ti + xi), (sr - ur, si - ui), (tr - xr, ti - xi)]


def radix16(vals, sign):
    inner = [radix4([vals[4 * n1 + n2] for n1 in range(4)], sign) for n2 in range(4)]
    out = [None] * 16
    for k1 in range(4):
        column = []
        for n2 in range(4):
            turn = n2 * k1
            value = inner[n2][k1]
            if turn == 4:
                re, im = value
                value = (im, -re) if sign < 0 else (-im, re)
            elif turn == 2 or turn == 6:
                half = math.sqrt(0.5)
                re, im = value
                if sign < 0:
                    value = ((re + im) * half, (im - re) * half)
                else:
                    value = ((re - im) * half, (re + im) * half)
                if turn == 6:
                    re, im = value
                    value = (im, -re) if sign < 0 else (-im, re)
            elif turn:
                angle = sign * TWO_PI * turn / 16
                value = cmul_const(value, math.cos(angle), math.sin(angle))
            column.append(value)
        for k2, value in enumerate(radix4(column, sign)):
            out[k1 + 4 * k2] = value
    return out


def unit_phase(step):
    quarter = (step + 256) >> 9
    angle = (step - (quarter << 9)).astype(F32) * (TWO_PI / SIDE)
    square = angle * angle
    sine = angle * (
        1.0
        + square
        * (-1.6666654611e-1 + square * (8.3321608736e-3 + square * -1.9515295891e-4))
    )
    cosine = 1.0 + square * (
        -0.5
        + square
        * (4.166664568298827e-2 + square * (-1.388731625493765e-3 + square * 2.443315711809948e-5))
    )
    odd = (quarter & 1) == 1
    cos_mag = jnp.where(odd, sine, cosine)
    sin_mag = jnp.where(odd, cosine, sine)
    cos_val = jnp.where(((quarter + 1) & 2) == 2, -cos_mag, cos_mag)
    sin_val = jnp.where((quarter & 2) == 2, -sin_mag, sin_mag)
    return cos_val, sin_val


def pick_lanes(value, index):
    numbers = lax.GatherDimensionNumbers(
        offset_dims=(),
        collapsed_slice_dims=(1,),
        start_index_map=(1,),
        operand_batching_dims=(0,),
        start_indices_batching_dims=(0,),
    )
    return lax.gather(
        value,
        index[..., None],
        numbers,
        slice_sizes=(1, 1),
        mode=lax.GatherScatterMode.PROMISE_IN_BOUNDS,
    )


def lane_block(shape):
    return lax.broadcasted_iota(jnp.int32, shape, 1) >> 5


def slots_to_pairs(blocks):
    where = lane_block(blocks[0].shape)
    rows = []
    for turn in range(4):
        total = None
        for member in range(4):
            shift = 32 * (member - turn) % 128
            moved = pltpu.roll(blocks[member], shift, 1) if shift else blocks[member]
            total = moved if total is None else jnp.where(where == member, moved, total)
        rows.append(total)
    return rows


def pairs_to_slots(rows):
    where = lane_block(rows[0].shape)
    blocks = []
    for member in range(4):
        total = None
        for turn in range(4):
            shift = 32 * (turn - member) % 128
            moved = pltpu.roll(rows[turn], shift, 1) if shift else rows[turn]
            total = moved if total is None else jnp.where(where == turn, moved, total)
        blocks.append(total)
    return blocks


def wide_row(block):
    return jnp.concatenate([block[k : k + 1, :] for k in range(block.shape[0])], axis=1)


def tall_block(row):
    count = row.shape[1] // 128
    return jnp.concatenate([row[:, 128 * k : 128 * (k + 1)] for k in range(count)], axis=0)


def jones_outer(left, right):
    real_rows = []
    imag_rows = []
    for row_a in range(2):
        for row_b in range(2):
            real_sum = 0.0
            imag_sum = 0.0
            for inner in range(2):
                left_re = left[row_a * 2 + inner]
                left_im = left[4 + row_a * 2 + inner]
                right_re = right[row_b * 2 + inner]
                right_im = right[4 + row_b * 2 + inner]
                real_sum = real_sum + left_re * right_re + left_im * right_im
                imag_sum = imag_sum + left_im * right_re - left_re * right_im
            real_rows.append(real_sum)
            imag_rows.append(imag_sum)
    return jnp.concatenate(real_rows, axis=0), jnp.concatenate(imag_rows, axis=0)


def jones_stokes(left, right, resid):
    total_re = 0.0
    total_im = 0.0
    for inner in range(2):
        for row_a in range(2):
            for row_b in range(2):
                left_re = left[row_a * 2 + inner]
                left_im = left[4 + row_a * 2 + inner]
                res_re = resid[row_a * 2 + row_b]
                res_im = resid[4 + row_a * 2 + row_b]
                right_re = right[row_b * 2 + inner]
                right_im = right[4 + row_b * 2 + inner]
                mid_re = left_re * res_re + left_im * res_im
                mid_im = left_re * res_im - left_im * res_re
                total_re = total_re + mid_re * right_re - mid_im * right_im
                total_im = total_im + mid_re * right_im + mid_im * right_re
    return 0.5 * total_re, 0.5 * total_im


def exchange_kernel(
    n_vis,
    n_facet,
    vis_hbm,
    weight_hbm,
    live_hbm,
    station_p_hbm,
    station_q_hbm,
    interval_hbm,
    cell_row_hbm,
    cell_col_hbm,
    gain_hbm,
    image_hbm,
    turn_hbm,
    twist_hbm,
    resid_ref,
    table,
    turn_ref,
    twist_ref,
    vis_ref,
    weight_ref,
    live_ref,
    station_p_ref,
    station_q_ref,
    interval_ref,
    cell_row_ref,
    cell_col_ref,
    gain_ref,
    image_ref,
    gain_all,
    part_out,
    part_in,
    pred_in,
    stokes_in,
    lines,
    work_re,
    work_im,
    local_row,
    local_col,
    values,
    step_cos,
    step_sin,
    fine_cos,
    fine_sin,
    load_sem,
    gain_send,
    gain_recv,
    gain_pair_send,
    gain_pair_recv,
    part_send,
    part_recv,
    pred_send,
    pred_recv,
    stokes_send,
    stokes_recv,
):
    me = lax.axis_index("vis")
    facet = lax.axis_index("facet")
    side_x = image_ref.shape[0]
    width = values.shape[3]
    slots = vis_ref.shape[1]
    parts, rows_k = part_in.shape[0], part_in.shape[2] // 2
    part = slots // parts
    part_pairs = RADIX // parts

    order = (
        (cell_row_hbm, cell_row_ref),
        (cell_col_hbm, cell_col_ref),
        (gain_hbm, gain_ref),
        (image_hbm, image_ref),
        (turn_hbm, turn_ref),
        (twist_hbm, twist_ref),
        (interval_hbm, interval_ref),
        (station_p_hbm, station_p_ref),
        (station_q_hbm, station_q_ref),
        (live_hbm, live_ref),
        (weight_hbm, weight_ref),
        (vis_hbm, vis_ref),
    )
    loads = [
        pltpu.make_async_copy(source, target, load_sem.at[place])
        for place, (source, target) in enumerate(order)
    ]
    for load in loads:
        load.start()

    ring_z, ring_y = n_vis // 4, n_facet // 2
    side, own_z, own_core = me // (2 * ring_z), (me // 2) & (ring_z - 1), me & 1
    own_y, own_x = facet // 2, facet & 1
    vis_steps = [
        (away, along, core)
        for away in range(2)
        for along in range(ring_z)
        for core in range(2)
        if (away, along, core) != (0, 0, 0)
    ]
    vis_steps.sort(key=lambda step: (-2 * step[0] - min(step[1], ring_z - step[1]), -step[2]))
    facet_steps = [(along, away) for along in range(ring_y) for away in range(2) if along or away]
    facet_steps.sort(key=lambda step: -min(step[0], ring_y - step[0]) - step[1])

    def vis_peer(step):
        away, along, core = step
        z = (own_z + along) & (ring_z - 1) if along else own_z
        return ((side ^ away) * ring_z + z) * 2 + (own_core ^ core)

    def facet_peer(step):
        along, away = step
        y = (own_y + along) & (ring_y - 1) if along else own_y
        return y * 2 + (own_x ^ away)

    barrier = pltpu.get_barrier_semaphore()
    for step in vis_steps:
        pl.semaphore_signal(barrier, 1, device_id=(vis_peer(step), facet), device_id_type=MESH)
    for step in facet_steps:
        pl.semaphore_signal(barrier, 1, device_id=(me, facet_peer(step)), device_id_type=MESH)

    def send_all(source, target, send_sem, recv_sem):
        for step in vis_steps:
            peer = vis_peer(step)
            pltpu.make_async_remote_copy(
                src_ref=source(peer),
                dst_ref=target.at[me],
                send_sem=send_sem,
                recv_sem=recv_sem(step),
                device_id=(peer, facet),
                device_id_type=MESH,
            ).start()

    def wait_blocks(buffer, count, sem):
        view = buffer.at[pl.ds(0, count)]
        pltpu.make_async_copy(view, view, sem).wait()

    def pair_row(pair):
        return lax.rem(pair, 4) * 4 + pair // 4

    loads[0].wait()
    loads[1].wait()

    def group_place(group):
        return group // 4, pl.ds(pl.multiple_of(lax.rem(group, 4) * 128, 128), 128)

    def order_cells(group, carry):
        place, lanes = group_place(group)

        def read(holder):
            rows = pl.ds(holder * 4, 4)
            return jnp.concatenate([cell_row_ref[rows, :], cell_col_ref[rows, :]], axis=0)

        for turn, rows in enumerate(slots_to_pairs([read(4 * group + k) for k in range(4)])):
            lane = lax.broadcasted_iota(jnp.int32, (4, 128), 1)
            local_row[place, 4 * turn : 4 * turn + 4, lanes] = rows[0:4] + ((lane >> 4) & 1) * 64
            local_col[place, 4 * turn : 4 * turn + 4, lanes] = rows[4:8]
        return carry

    lax.fori_loop(0, n_vis // 4, order_cells, 0, unroll=4)
    for place in range(2):
        cos, sin = unit_phase((local_col[place] * 8) & (SIDE - 1))
        step_cos[place] = cos
        step_sin[place] = sin

    loads[2].wait()
    intervals_here = gain_ref.shape[1]
    stations = gain_ref.shape[2]
    core, chip = me & 1, me // 2
    gain_all[core, chip] = jnp.zeros((8, 256), F32)
    for comp in range(8):
        half, lane = comp // 4, 64 * (comp % 4)
        rows = slice(4 * half, 4 * half + intervals_here)
        gain_all[core, chip, rows, lane : lane + stations] = gain_ref[comp]

    loads[3].wait()
    lines[...] = image_ref[...].T
    loads[4].wait()
    loads[5].wait()
    first_hi = jnp.concatenate([turn_ref[:INNER], turn_ref[INNER : 2 * INNER]], axis=1)
    first_lo = jnp.concatenate([turn_ref[2 * INNER : 3 * INNER], turn_ref[3 * INNER :]], axis=1)
    first_twice = jnp.concatenate([first_hi, first_hi], axis=0)
    group_b = 8
    for start in range(0, RADIX, group_b):
        halves = [
            split_pair(lines[pl.ds(b, INNER, stride=RADIX), :].T)
            for b in range(start, start + group_b)
        ]
        high = jnp.concatenate([pair[0] for pair in halves], axis=0)
        low = jnp.concatenate([pair[1] for pair in halves], axis=0)
        both = matmul(jnp.concatenate([high, low], axis=1), first_twice) + matmul(high, first_lo)
        for place in range(group_b):
            b = start + place
            here = both[place * side_x : (place + 1) * side_x]
            re, im = here[:, :INNER], here[:, INNER:]
            cos = twist_ref[0, b : b + 1, :]
            sin = twist_ref[1, b : b + 1, :]
            work_re[b] = re * cos + im * sin
            work_im[b] = im * cos - re * sin

    def forward_rows(chunk, carry):
        rows = pl.ds(pl.multiple_of(chunk * 8, 8), 8)
        rows_im = pl.ds(pl.multiple_of(side_x + chunk * 8, 8), 8)
        vals = radix16([(work_re[b, rows, :], work_im[b, rows, :]) for b in range(RADIX)], -1.0)
        for q in range(RADIX):
            table[q, rows, :] = vals[q][0]
            table[q, rows_im, :] = vals[q][1]
        return carry

    lax.fori_loop(0, side_x // 8, forward_rows, 0, unroll=4)

    pl.semaphore_wait(barrier, n_vis + n_facet - 2)
    for step in vis_steps:
        if step[2] == 0:
            pltpu.make_async_remote_copy(
                src_ref=gain_all.at[core, chip],
                dst_ref=gain_all.at[core, chip],
                send_sem=gain_send.at[0],
                recv_sem=gain_recv.at[step[0]],
                device_id=(vis_peer(step), facet),
                device_id_type=MESH,
            ).start()

    chunk_w = 512
    by_lanes = 256
    blocks_x = side_x // 8

    def hot_columns(local):
        index = lax.broadcasted_iota(jnp.int32, (INNER, local.shape[1]), 0)
        return jnp.where(index == local, 1.0, 0.0).astype(BF16)

    def value_row(pair):
        return lax.rem(pair, 4) * 2 * rows_k + lax.rem(pair // 4, rows_k)

    def forward_pair(pair, carry):
        half = pair // part_pairs
        row = pl.ds(pair_row(pair), 1)
        high, low = split_pair(table[pair])
        both = jnp.concatenate([high, low], axis=0)

        def picked_by_matmul(local):
            picked = matmul(both, hot_columns(local))
            picked = picked[: 2 * side_x] + picked[2 * side_x :]
            return lambda first: picked[first : first + 8]

        def picked_by_lanes(local):
            index = jnp.broadcast_to(local, (8, INNER))
            return lambda first: pick_lanes(table[pair, first : first + 8, :], index)

        pieces = [(start, INNER, picked_by_lanes) for start in range(0, by_lanes, INNER)]
        pieces += [(start, 256, picked_by_matmul) for start in range(by_lanes, width, 256)]
        for place in range(2):
            out_re = []
            out_im = []
            whole_index = local_row[place, row, :]
            whole_cos = step_cos[place, row, :]
            whole_sin = step_sin[place, row, :]
            x_index = me * side_x + lax.broadcasted_iota(jnp.int32, (8, width), 0)
            all_cos, all_sin = unit_phase((local_col[place, row, :] * x_index) & (SIDE - 1))
            fine_cos[pair, place] = all_cos
            fine_sin[pair, place] = all_sin
            for start, size, picker in pieces:
                lanes = slice(start, start + size)
                pick = picker(whole_index[:, lanes])
                cos = jnp.broadcast_to(whole_cos[:, lanes], (8, size))
                sin = jnp.broadcast_to(whole_sin[:, lanes], (8, size))
                sum_re = pick(8 * blocks_x - 8)
                sum_im = pick(side_x + 8 * blocks_x - 8)
                for block in range(blocks_x - 2, -1, -1):
                    re = pick(8 * block)
                    im = pick(side_x + 8 * block)
                    sum_re, sum_im = (
                        re + (sum_re * cos + sum_im * sin),
                        im + (sum_im * cos - sum_re * sin),
                    )
                cos = all_cos[:, lanes]
                sin = all_sin[:, lanes]
                out_re.append(jnp.sum(sum_re * cos + sum_im * sin, axis=0, keepdims=True))
                out_im.append(jnp.sum(sum_im * cos - sum_re * sin, axis=0, keepdims=True))
            re_row = pl.ds(value_row(pair), 1)
            im_row = pl.ds(value_row(pair) + rows_k, 1)
            values[half, place, re_row, :] = jnp.concatenate(out_re, axis=1)
            values[half, place, im_row, :] = jnp.concatenate(out_im, axis=1)
        return carry

    for half in range(parts):
        lax.fori_loop(
            part_pairs * half, part_pairs * (half + 1), forward_pair, 0, unroll=min(8, part_pairs)
        )

        def pack_values(group, carry):
            place, lanes = group_place(group)
            rows = [
                values[half, place, 2 * rows_k * turn : 2 * rows_k * (turn + 1), lanes]
                for turn in range(4)
            ]
            for member, block in enumerate(pairs_to_slots(rows)):
                part_out[half, 4 * group + member] = block
            return carry

        lax.fori_loop(0, n_vis // 4, pack_values, 0, unroll=8)
        send_all(
            lambda peer: part_out.at[half, peer],
            part_in.at[half],
            part_send.at[half],
            lambda step: part_recv.at[half],
        )
        part_in[half, me] = part_out[half, me]

    for load in loads[6:]:
        load.wait()
    interval = wide_row(interval_ref[...])
    holder = interval >> 2
    gain_row = ((holder & 1) * (n_vis // 2) + (holder >> 1)) * 8 + (interval & 3)
    station = lax.broadcasted_iota(jnp.int32, (64, slots), 0)
    at_p = jnp.where(station == wide_row(station_p_ref[...]), 1.0, 0.0)
    at_q = jnp.where(station == wide_row(station_q_ref[...]), 1.0, 0.0)
    index = lax.broadcasted_iota(jnp.int32, (n_vis * 8, slots), 0)
    hots = [
        jnp.where(index == gain_row + 4 * half, 1.0, 0.0).astype(BF16) for half in range(2)
    ]
    live = wide_row(live_ref[...]).astype(F32)
    scale = wide_row(weight_ref[...]) * live
    to_other_core = []
    for away in range(2):
        wait_blocks(gain_all.at[core], ring_z - 1 + away, gain_recv.at[away])
        chips = pl.ds((side ^ away) * ring_z, ring_z)
        to_other_core.append(
            pltpu.make_async_remote_copy(
                src_ref=gain_all.at[core, chips],
                dst_ref=gain_all.at[core, chips],
                send_sem=gain_pair_send.at[away],
                recv_sem=gain_pair_recv.at[away],
                device_id=(me ^ 1, facet),
                device_id_type=MESH,
            )
        )
        to_other_core[-1].start()
    for away in range(2):
        wait_blocks(gain_all.at[1 - core], ring_z, gain_pair_recv.at[away])
    high, low = split_pair(gain_all[...].reshape(n_vis * 8, 256).T)
    both = jnp.concatenate([high, low], axis=0)
    jones_p = []
    jones_q = []
    for half in range(2):
        picked = matmul(both, hots[half])
        picked = picked[:256] + picked[256:]
        for comp in range(4):
            here = picked[64 * comp : 64 * comp + 64]
            jones_p.append(jnp.sum(here * at_p, axis=0, keepdims=True))
            jones_q.append(jnp.sum(here * at_q, axis=0, keepdims=True))
    outer_re, outer_im = jones_outer(jones_p, jones_q)

    for half in range(parts):
        here = slice(half * part, (half + 1) * part)
        wait_blocks(part_in.at[half], n_vis - 1, part_recv.at[half])
        model = jnp.sum(part_in[half], axis=0) * (1.0 / SIDE)
        model_re = wide_row(model[:rows_k])
        model_im = wide_row(model[rows_k:])
        own_re, own_im = outer_re[:, here], outer_im[:, here]
        pred_in[half, facet, 0:4, :] = model_re * own_re - model_im * own_im
        pred_in[half, facet, 4:8, :] = model_re * own_im + model_im * own_re

        for step in facet_steps:
            pltpu.make_async_remote_copy(
                src_ref=pred_in.at[half, facet],
                dst_ref=pred_in.at[half, facet],
                send_sem=pred_send.at[half],
                recv_sem=pred_recv.at[half],
                device_id=(me, facet_peer(step)),
                device_id_type=MESH,
            ).start()

    for half in range(parts):
        here = slice(half * part, (half + 1) * part)
        wait_blocks(pred_in.at[half], n_facet - 1, pred_recv.at[half])
        predicted = pred_in[half, 0]
        for other in range(1, n_facet):
            predicted = predicted + pred_in[half, other]
        resid = (vis_ref[:, here] - predicted) * live[:, here]
        resid_ref[:, here] = resid
        stokes_re, stokes_im = jones_stokes(
            [gain[:, here] for gain in jones_p],
            [gain[:, here] for gain in jones_q],
            [resid[comp : comp + 1] for comp in range(8)],
        )
        stokes_in[half, me, :rows_k, :] = tall_block(stokes_re * scale[:, here])
        stokes_in[half, me, rows_k:, :] = tall_block(stokes_im * scale[:, here])
        send_all(
            lambda peer: stokes_in.at[half, me],
            stokes_in.at[half],
            stokes_send.at[half],
            lambda step: stokes_recv.at[half, step[0]],
        )

    def backward_pair(pair, place, first):
        total = jnp.zeros((4 * side_x, INNER), F32)
        half = pair // part_pairs
        row = pl.ds(pair_row(pair), 1)
        whole_re = values[half, place, pl.ds(value_row(pair), 1), :]
        whole_im = values[half, place, pl.ds(value_row(pair) + rows_k, 1), :]
        whole_index = local_row[place, row, :]
        whole_cos = step_cos[place, row, :]
        whole_sin = step_sin[place, row, :]
        for start in range(0, width, chunk_w):
            lanes = slice(start, start + chunk_w)
            re = whole_re[:, lanes]
            im = whole_im[:, lanes]
            cos = fine_cos[pair, place, :, lanes]
            sin = fine_sin[pair, place, :, lanes]
            real_rows = [re * cos - im * sin]
            imag_rows = [re * sin + im * cos]
            cos = jnp.broadcast_to(whole_cos[:, lanes], (8, chunk_w))
            sin = jnp.broadcast_to(whole_sin[:, lanes], (8, chunk_w))
            for _ in range(blocks_x - 1):
                re, im = real_rows[-1], imag_rows[-1]
                real_rows.append(re * cos - im * sin)
                imag_rows.append(re * sin + im * cos)
            high, low = split_pair(jnp.concatenate(real_rows + imag_rows, axis=0))
            both = jnp.concatenate([high, low], axis=0)
            total = total + lax.dot_general(
                both,
                hot_columns(whole_index[:, lanes]),
                (((1,), (1,)), ((), ())),
                preferred_element_type=F32,
            )
        total = total[: 2 * side_x] + total[2 * side_x :]
        table[pair] = total if first else table[pair] + total

    for half in range(parts):
        for away in range(2):
            place = side ^ away
            count = n_vis // 2 - (1 - away)
            wait_blocks(stokes_in.at[half], count, stokes_recv.at[half, away])

            def order_stokes(group, carry):
                lanes = pl.ds(pl.multiple_of(group * 128, 128), 128)
                first = place * (n_vis // 2) + 4 * group
                blocks = [stokes_in[half, first + member] for member in range(4)]
                for turn, rows in enumerate(slots_to_pairs(blocks)):
                    values[half, place, 2 * rows_k * turn : 2 * rows_k * (turn + 1), lanes] = rows
                return carry

            def backward(pair, carry):
                backward_pair(pair, place, away == 0)
                return carry

            lax.fori_loop(0, n_vis // 8, order_stokes, 0, unroll=4)
            lax.fori_loop(
                part_pairs * half, part_pairs * (half + 1), backward, 0, unroll=min(8, part_pairs)
            )

    wait_blocks(gain_all.at[core], n_vis // 2 - 1, gain_send.at[0])
    for away in range(2):
        wait_blocks(gain_all.at[core], ring_z, gain_pair_send.at[away])
    for half in range(parts):
        wait_blocks(part_in.at[half], n_vis - 1, part_send.at[half])
        wait_blocks(pred_in.at[half], n_facet - 1, pred_send.at[half])
        wait_blocks(stokes_in.at[half], n_vis - 1, stokes_send.at[half])


def image_kernel(
    factor,
    resid_ref,
    table,
    turn_ref,
    twist_ref,
    resid_hbm,
    dirty_hbm,
    work_re,
    work_im,
    lines,
    dirty,
    resid_sem,
    dirty_sem,
):
    side_x = dirty.shape[0]
    keep = pltpu.make_async_copy(resid_ref, resid_hbm, resid_sem)
    keep.start()

    def backward_rows(chunk, carry):
        rows = pl.ds(pl.multiple_of(chunk * 8, 8), 8)
        rows_im = pl.ds(pl.multiple_of(side_x + chunk * 8, 8), 8)
        vals = radix16([(table[q, rows, :], table[q, rows_im, :]) for q in range(RADIX)], 1.0)
        for b in range(RADIX):
            re, im = vals[b]
            cos = twist_ref[0, b : b + 1, :]
            sin = twist_ref[1, b : b + 1, :]
            work_re[b, rows, :] = re * cos - im * sin
            work_im[b, rows, :] = re * sin + im * cos
        return carry

    lax.fori_loop(0, side_x // 8, backward_rows, 0, unroll=8)

    last_hi = turn_ref[: 2 * INNER]
    last_lo = turn_ref[2 * INNER :]
    last_both = jnp.concatenate([last_hi, last_lo], axis=1)
    group_b = 8
    for start in range(0, RADIX, group_b):
        halves = [
            split_pair(jnp.concatenate([work_re[b], work_im[b]], axis=1))
            for b in range(start, start + group_b)
        ]
        high = jnp.concatenate([pair[0] for pair in halves], axis=0)
        low = jnp.concatenate([pair[1] for pair in halves], axis=0)
        both = matmul(high, last_both)
        part = (both[:, :INNER] + (both[:, INNER:] + matmul(low, last_hi))) * factor
        for place in range(group_b):
            here = part[place * side_x : (place + 1) * side_x]
            lines[pl.ds(start + place, INNER, stride=RADIX), :] = here.T
    count = dirty_sem.shape[0]
    wide = SIDE // count
    copies = []
    for piece in range(count):
        here = slice(piece * wide, (piece + 1) * wide)
        dirty[:, here] = lines[here, :].T
        copies.append(
            pltpu.make_async_copy(dirty.at[:, here], dirty_hbm.at[:, here], dirty_sem.at[piece])
        )
        copies[-1].start()
    for copy in copies:
        copy.wait()
    keep.wait()


def per_device(
    visibilities,
    weights,
    live_slots,
    station_p,
    station_q,
    interval,
    cell_row,
    cell_col,
    jones_gains,
    model_image,
):
    n_vis = lax.axis_size("vis")
    n_facet = lax.axis_size("facet")
    side_x = model_image.shape[1]
    slots = visibilities.shape[1]
    width = n_vis * slots // RADIX // 2

    def rows_of(array):
        return array.reshape(-1, 128)

    turn, twist = [jnp.asarray(table) for table in make_tables()]
    given = [
        visibilities,
        rows_of(weights),
        rows_of(live_slots),
        rows_of(station_p),
        rows_of(station_q),
        rows_of(interval),
        rows_of(cell_row),
        rows_of(cell_col),
        jones_gains[0],
        model_image[0],
        turn,
        twist,
    ]
    in_hbm = pl.BlockSpec(memory_space=pltpu.HBM)
    in_vmem = pl.BlockSpec(memory_space=pltpu.VMEM)
    work = pltpu.VMEM((RADIX, side_x, INNER), F32)
    kept = pl.pallas_call(
        functools.partial(exchange_kernel, n_vis, n_facet),
        out_shape=(
            pltpu.VMEM((8, slots), F32),
            pltpu.VMEM((RADIX, 2 * side_x, INNER), F32),
            pltpu.VMEM(turn.shape, turn.dtype),
            pltpu.VMEM(twist.shape, twist.dtype),
        ),
        in_specs=[in_hbm] * len(given),
        out_specs=(in_vmem,) * 4,
        scratch_shapes=[pltpu.VMEM(array.shape, array.dtype) for array in given[:-2]]
        + [
            pltpu.VMEM((2, n_vis // 2, 8, 256), F32),
            pltpu.VMEM((PARTS, n_vis, 8 // PARTS, 128), F32),
            pltpu.VMEM((PARTS, n_vis, 8 // PARTS, 128), F32),
            pltpu.VMEM((PARTS, n_facet, 8, slots // PARTS), F32),
            pltpu.VMEM((PARTS, n_vis, 8 // PARTS, 128), F32),
            pltpu.VMEM((SIDE, side_x), F32),
            work,
            work,
            pltpu.VMEM((2, 16, width), jnp.int32),
            pltpu.VMEM((2, 16, width), jnp.int32),
            pltpu.VMEM((PARTS, 2, 32 // PARTS, width), F32),
            pltpu.VMEM((2, 16, width), F32),
            pltpu.VMEM((2, 16, width), F32),
            pltpu.VMEM((RADIX, 2, 8, width), F32),
            pltpu.VMEM((RADIX, 2, 8, width), F32),
            pltpu.SemaphoreType.DMA((len(given),)),
        ]
        + [pltpu.SemaphoreType.DMA((2,))] * 4
        + [pltpu.SemaphoreType.DMA((PARTS,))] * 5
        + [pltpu.SemaphoreType.DMA((PARTS, 2))],
        compiler_params=pltpu.CompilerParams(
            collective_id=0, has_side_effects=True, vmem_limit_bytes=40 * 1024 * 1024
        ),
    )(*[pltpu.with_memory_space_constraint(array, pltpu.HBM) for array in given])
    resid, dirty = pl.pallas_call(
        functools.partial(image_kernel, 4.0 / math.sqrt(slots * n_vis)),
        out_shape=(
            pltpu.HBM((8, slots), F32),
            pltpu.HBM((side_x, SIDE), F32),
        ),
        in_specs=[in_vmem] * 4,
        out_specs=(in_hbm, in_hbm),
        scratch_shapes=[
            work,
            work,
            pltpu.VMEM((SIDE, side_x), F32),
            pltpu.VMEM((side_x, SIDE), F32),
            pltpu.SemaphoreType.DMA(()),
            pltpu.SemaphoreType.DMA((4,)),
        ],
        compiler_params=pltpu.CompilerParams(vmem_limit_bytes=40 * 1024 * 1024),
    )(*kept)
    return resid, dirty[None]


def solution(mesh):
    return jax.shard_map(
        per_device,
        mesh=mesh,
        in_specs=(
            P(None, "vis"),
            P("vis"),
            P("vis"),
            P("vis"),
            P("vis"),
            P("vis"),
            P(),
            P(),
            P("facet", None, "vis", None),
            P("facet", "vis", None),
        ),
        out_specs=(P(None, "vis"), P("facet", "vis", None)),
        check_vma=False,
    )
```
